512 devices in a mesh: feed: 8 (over y, z_hi), tm: 64 (over x, z_lo, core).
Axes of the slice: x: 4, y: 4, z: 16 (z_hi: 2, z_lo: 8; z = z_hi * 8 + z_lo), core: 2. Of those that a mesh axis runs over, the one named last changes fastest.
Arguments:
- voltages: bfloat16 [256, 524288], P('feed', 'tm'), may hold values from -6 to 6
- previous: bfloat16 [256, 30720], P('feed'), may hold values from -16 to 16
- filter_taps: float32 [16, 2048], replicated, may hold values from -1 to 1
Outputs:
- visibilities: float32 [2, 1024, 256, 256], P(None, 'tm', 'feed')
The draws below stay inside these ranges and needn't reach their ends.
All inputs are finite; a program needn't handle non-finite values.
Results may differ from the reference program's by a relative error of at most 0.0095.
Values may be sent and summed in bfloat16 or wider, within the bound.
No kernel may reach another device: no remote copies, remote signals or barrier semaphores. Data moves between devices by JAX's collectives and lax.ppermute only.
A program may use at most 64 MiB of HBM per device.

```python
import math
from functools import partial
import jax
import jax.numpy as jnp
from jax import lax

NI = 256
FFT = 2048
NC = 1024
TAPS = 16
SPECTRA = 256
SAMPLES = 524288
HISTORY = 30720


def levels(own_key, shape, cuts, low, top_value):
    gain, own = 1.0, jax.random.fold_in(own_key, 6)
    for position, blocks in cuts:
        draws = jnp.exp(jax.random.uniform(jax.random.fold_in(own, position), (blocks,), jnp.float32, low / len(cuts), top_value / len(cuts)))
        gain = gain * jnp.repeat(draws, shape[position] // blocks).reshape([-1 if axis == position else 1 for axis in range(len(shape))])
    return gain


def normal_values(key, dims, deviation, limit, split=(), kind=jnp.bfloat16):
    array = deviation * jax.random.normal(key, dims, jnp.float32)
    if split:
        array = array * levels(key, dims, split, -0.22, 0.18)
    return jnp.clip(array, -limit, limit).astype(kind)


def setup_inputs(seed: int = 0) -> dict:
    splits = jax.random.split(jax.random.key(seed), 4)
    voltages = normal_values(splits[0], (NI, SAMPLES), 1.0, 6.0, ((0, 8), (1, 64)))
    previous = normal_values(splits[1], (NI, HISTORY), 4.0, 16.0, ((0, 8),))
    filter_taps = normal_values(splits[2], (TAPS, FFT), 0.25, 1.0, (), jnp.float32)
    return {"voltages": voltages, "previous": previous, "filter_taps": filter_taps}


def channelize(block_pair, filter_taps):
    fresh, earlier = block_pair
    count = fresh.shape[0]
    extended = jnp.concatenate([earlier, fresh], axis=1).reshape(count, TAPS - 1 + SPECTRA, FFT)
    filtered = jnp.zeros((count, SPECTRA, FFT), jnp.float32)
    for tap_index in range(TAPS):
        filtered = filtered + filter_taps[tap_index] * extended[:, tap_index:tap_index + SPECTRA].astype(jnp.float32)
    rounded = lax.optimization_barrier(filtered.astype(jnp.bfloat16)).astype(jnp.float32)
    spectrum = jnp.fft.rfft(rounded, axis=-1)[..., :NC]
    scaling = 1.0 / math.sqrt(FFT)
    return ((jnp.real(spectrum) * scaling).astype(jnp.bfloat16), (jnp.imag(spectrum) * scaling).astype(jnp.bfloat16))

def correlate_block(block_pair):
    first_set = block_pair[0].astype(jnp.float32)
    second_set = block_pair[1].astype(jnp.float32)
    real_sum = jnp.einsum('cis,cjs->cij', first_set, first_set) + jnp.einsum('cis,cjs->cij', second_set, second_set)
    imag_sum = jnp.einsum('cis,cjs->cij', second_set, first_set) - jnp.einsum('cis,cjs->cij', first_set, second_set)
    return jnp.stack([real_sum, imag_sum])

def reference(voltages, previous, filter_taps):
    groups = NI // 8
    real_part, imag_part = lax.map(partial(channelize, filter_taps=filter_taps), (voltages.reshape(groups, 8, SAMPLES), previous.reshape(groups, 8, HISTORY)))
    real_part = real_part.reshape(NI, SPECTRA, NC).transpose(2, 0, 1).reshape(NC // 8, 8, NI, SPECTRA)
    imag_part = imag_part.reshape(NI, SPECTRA, NC).transpose(2, 0, 1).reshape(NC // 8, 8, NI, SPECTRA)
    result = lax.map(correlate_block, (real_part, imag_part))
    return result.transpose(1, 0, 2, 3, 4).reshape(2, NC, NI, NI) * (1.0 / SPECTRA)
```

```python
import functools
import math

import jax
import jax.numpy as jnp
import ml_dtypes
import numpy as np
from jax import lax
from jax.experimental import pallas as pl
from jax.experimental.pallas import tpu as pltpu
from jax.sharding import PartitionSpec as P

FRAME = 2048
HALF = FRAME // 2
TAPS = 16
REACH = TAPS - 1
STEPS = 8


def dft_table(feeds, times):
    per_time = HALF // times
    per_device = per_time // feeds
    feed = np.arange(feeds).reshape(feeds, 1, 1)
    time = np.arange(times).reshape(1, times, 1)
    own = np.arange(per_device).reshape(1, 1, per_device)
    channel = (time * per_time + feed * per_device + own).reshape(-1)
    turns = (channel[:, None] * np.arange(FRAME)[None, :]) % FRAME
    angle = turns * (2.0 * math.pi / FRAME)
    table = np.stack([np.cos(angle), -np.sin(angle)], axis=1)
    return table.reshape(2 * HALF, FRAME).astype(ml_dtypes.bfloat16)


def channelize_kernel(first_ref, current, back1, back2, back3, back4, previous, taps, table, out, filtered):
    inputs, block = current.shape
    here = block // FRAME

    @pl.when(pl.program_id(0) == 0)
    def _():
        first = first_ref[0]

        def columns(j, carry):
            lane = pl.multiple_of(j * 128, 128)
            weights = [taps[t : t + 1, pl.ds(lane, 128)] for t in range(TAPS)]
            for row in range(0, inputs, 16):
                rows = pl.ds(row, 16)
                frames = []
                for e in range(REACH):
                    back = (REACH - e + here - 1) // here
                    source = (back1, back2, back3, back4)[back - 1]
                    at = source.shape[1] - (REACH - e - (back - 1) * here) * FRAME
                    moved = source[rows, pl.ds(pl.multiple_of(at + lane, 128), 128)].astype(jnp.float32)
                    held = jnp.minimum(first + e, REACH - 1) * FRAME + lane
                    old = previous[rows, pl.ds(pl.multiple_of(held, 128), 128)].astype(jnp.float32)
                    frames.append(jnp.where(first + e < REACH, old, moved))
                for s in range(here):
                    frames.append(current[rows, pl.ds(pl.multiple_of(s * FRAME + lane, 128), 128)].astype(jnp.float32))
                for s in range(here):
                    total = weights[0] * frames[s]
                    for t in range(1, TAPS):
                        total = total + weights[t] * frames[s + t]
                    filtered[pl.ds(s * inputs + row, 16), pl.ds(lane, 128)] = total.astype(jnp.bfloat16)
            return carry

        lax.fori_loop(0, FRAME // 128, columns, 0)

    spectrum = lax.dot_general(
        table[...], filtered[...], (((1,), (1,)), ((), ())), preferred_element_type=jnp.float32
    )
    out[...] = (spectrum * (1.0 / math.sqrt(FRAME))).astype(jnp.bfloat16)


def channelize(first, current, backs, previous, taps, table):
    inputs, block = current.shape
    rows = inputs * (block // FRAME)
    whole = lambda a: pl.BlockSpec(a.shape, lambda i: (0,) * a.ndim)
    step = table.shape[0] // STEPS
    operands = (current, *backs, previous, taps)
    return pl.pallas_call(
        channelize_kernel,
        grid=(STEPS,),
        out_shape=jax.ShapeDtypeStruct((table.shape[0], rows), jnp.bfloat16),
        in_specs=[pl.BlockSpec(memory_space=pltpu.SMEM)]
        + [whole(a) for a in operands]
        + [pl.BlockSpec((step, FRAME), lambda i: (i, 0))],
        out_specs=pl.BlockSpec((step, rows), lambda i: (i, 0)),
        scratch_shapes=[pltpu.VMEM((rows, FRAME), jnp.bfloat16)],
        compiler_params=pltpu.CompilerParams(vmem_limit_bytes=40 * 2**20),
    )(first, *operands, table)


def correlate_kernel(feeds, inputs, scale, received, out, z_ref, w_ref):
    channels, rows, lanes = received.shape
    wide = rows // feeds
    spectra = lanes // inputs
    sign = jnp.where(lax.broadcasted_iota(jnp.int32, (inputs, wide), 1) < wide // 2, 1.0, -1.0)
    for k in range(channels):
        for f in range(feeds):
            turned = received[k, f * wide : (f + 1) * wide, :].astype(jnp.float32).T
            for s in range(spectra):
                part = turned[s * inputs : (s + 1) * inputs]
                at = (slice(f * inputs, (f + 1) * inputs), slice(s * wide, (s + 1) * wide))
                z_ref[at] = part.astype(jnp.bfloat16)
                w_ref[at] = (pltpu.roll(part, wide // 2, 1) * sign).astype(jnp.bfloat16)
        every = z_ref[...]
        for part, left in enumerate((z_ref, w_ref)):
            sums = lax.dot_general(
                left[...], every, (((1,), (1,)), ((), ())), preferred_element_type=jnp.float32
            )
            sums = (sums * scale).astype(jnp.bfloat16)
            for f in range(feeds):
                out[f, part, k] = sums[f * inputs : (f + 1) * inputs]


def correlate(received, feeds, inputs, scale):
    channels, rows, lanes = received.shape
    total = feeds * inputs
    depth = rows // feeds * (lanes // inputs)
    return pl.pallas_call(
        functools.partial(correlate_kernel, feeds, inputs, scale),
        out_shape=jax.ShapeDtypeStruct((feeds, 2, channels, inputs, total), jnp.bfloat16),
        scratch_shapes=[pltpu.VMEM((total, depth), jnp.bfloat16)] * 2,
        compiler_params=pltpu.CompilerParams(vmem_limit_bytes=32 * 2**20),
    )(received)


def body(table, voltages, previous, filter_taps):
    inputs, block = voltages.shape
    here = block // FRAME
    feeds, times = lax.axis_size("feed"), lax.axis_size("tm")
    count_back = (REACH + here - 1) // here
    backs = []
    for distance in range(1, count_back + 1):
        count = min(here, REACH - (distance - 1) * here)
        route = [(i - distance, i) for i in range(distance, times)]
        backs.append(lax.ppermute(voltages[:, (here - count) * FRAME :], "tm", route))
    first = (lax.axis_index("tm") * here).astype(jnp.int32).reshape(1)
    spectra = channelize(first, voltages, backs, previous, filter_taps, table)
    rows = spectra.shape[1]
    own = HALF // (feeds * times)
    received = lax.all_to_all(
        spectra.reshape(feeds * times, own * 2, rows), ("feed", "tm"), 0, 0, tiled=True
    )
    received = received.reshape(feeds, times, own, 2, rows).transpose(2, 0, 3, 1, 4)
    received = received.reshape(own, feeds * 2 * times, rows)
    result = correlate(received, feeds, inputs, 1.0 / (times * here))
    result = lax.all_to_all(result, "feed", 0, 0, tiled=True)
    result = result.transpose(1, 0, 2, 3, 4).astype(jnp.float32)
    return result.reshape(2, feeds * own, inputs, feeds * inputs)


def solution(mesh):
    sizes = dict(mesh.shape)
    table = dft_table(sizes["feed"], sizes["tm"])
    placed = (P("feed", "tm"), P("feed", None), P())

    def run(voltages, previous, filter_taps):
        return jax.shard_map(
            functools.partial(body, jnp.asarray(table)),
            mesh=mesh,
            in_specs=placed,
            out_specs=P(None, "tm", "feed", None),
            check_vma=False,
        )(voltages, previous, filter_taps)

    return run
```

```python
import functools
import math

import jax
import jax.numpy as jnp
import ml_dtypes
import numpy as np
from jax import lax
from jax.experimental import pallas as pl
from jax.experimental.pallas import tpu as pltpu
from jax.sharding import PartitionSpec as P

FRAME = 2048
HALF = FRAME // 2
TAPS = 16
REACH = TAPS - 1
STEPS = 8
CORES = 2
VMEM_BYTES = 60 * 2**20


def dft_table(feeds, times):
    per_time = HALF // times
    per_device = per_time // feeds
    feed = np.arange(feeds).reshape(feeds, 1, 1)
    time = np.arange(times).reshape(1, times, 1)
    own = np.arange(per_device).reshape(1, 1, per_device)
    channel = (time * per_time + feed * per_device + own).reshape(-1)
    turns = (channel[:, None] * np.arange(FRAME)[None, :]) % FRAME
    angle = turns * (2.0 * math.pi / FRAME)
    table = np.stack([np.cos(angle), -np.sin(angle)], axis=1)
    return table.reshape(2 * HALF, FRAME).astype(ml_dtypes.bfloat16)


def channelize_kernel(place_ref, left, own, right, previous, taps, table, out, filtered):
    cores, inputs, block = own.shape
    here = block // FRAME
    spectra = cores * here
    back = REACH - spectra

    @pl.when(pl.program_id(0) == 0)
    def _():
        chip = place_ref[0]
        at_start = chip == 0
        at_end = chip == place_ref[1] - 1
        first_input = pl.multiple_of(place_ref[2], inputs)

        def columns(j, carry):
            lane = pl.multiple_of(j * 128, 128)
            weights = [taps[t : t + 1, pl.ds(lane, 128)] for t in range(TAPS)]
            frames = []
            for w in range(spectra + REACH):
                source = (left, own, right)[(w + spectra - back) // spectra]
                frame = (w + spectra - back) % spectra
                at = pl.ds(pl.multiple_of(frame % here * FRAME + lane, 128), 128)
                value = source[frame // here, :, at].astype(jnp.float32)
                if w < REACH:
                    held = w if w >= back else jnp.where(at_start, w + spectra, w)
                    at = pl.ds(pl.multiple_of(held * FRAME + lane, 128), 128)
                    old = previous[pl.ds(first_input, inputs), at].astype(jnp.float32)
                    use_old = at_end if w >= back else jnp.logical_or(at_start, at_end)
                    value = jnp.where(use_old, old, value)
                frames.append(value)
            for s in range(spectra):
                total = weights[0] * frames[s]
                for t in range(1, TAPS):
                    total = total + weights[t] * frames[s + t]
                filtered[pl.ds(s * inputs, inputs), pl.ds(lane, 128)] = total.astype(jnp.bfloat16)
            return carry

        lax.fori_loop(0, FRAME // 128, columns, 0)

    spectrum = lax.dot_general(
        table[...], filtered[...], (((1,), (1,)), ((), ())), preferred_element_type=jnp.float32
    )
    out[...] = (spectrum * (1.0 / math.sqrt(FRAME))).astype(jnp.bfloat16)


def channelize(place, left, own, right, previous, taps, table):
    cores, inputs, block = own.shape
    rows = cores * inputs * (block // FRAME)
    whole = lambda a: pl.BlockSpec(a.shape, lambda i: (0,) * a.ndim)
    step = table.shape[0] // STEPS
    operands = (left, own, right, previous, taps)
    return pl.pallas_call(
        channelize_kernel,
        grid=(STEPS,),
        out_shape=jax.ShapeDtypeStruct((table.shape[0], rows), jnp.bfloat16),
        in_specs=[pl.BlockSpec(memory_space=pltpu.SMEM)]
        + [whole(a) for a in operands]
        + [pl.BlockSpec((step, FRAME), lambda i: (i, 0))],
        out_specs=pl.BlockSpec((step, rows), lambda i: (i, 0)),
        scratch_shapes=[pltpu.VMEM((rows, FRAME), jnp.bfloat16)],
        compiler_params=pltpu.CompilerParams(vmem_limit_bytes=VMEM_BYTES),
    )(place, *operands, table)


def correlate_kernel(feeds, inputs, scale, received, out, z_ref, w_ref):
    channels, rows, lanes = received.shape
    wide = rows // feeds
    quarter = wide // 4
    lane = lax.broadcasted_iota(jnp.int32, (inputs, wide), 1)
    sign = jnp.where(lane < wide // 2, 1.0, -1.0)
    low = lane % (2 * quarter) < quarter
    for k in range(channels):
        for f in range(feeds):
            turned = received[k, f * wide : (f + 1) * wide, :].astype(jnp.float32).T
            for pair in range(lanes // inputs // 2):
                even = turned[2 * pair * inputs : (2 * pair + 1) * inputs]
                odd = turned[(2 * pair + 1) * inputs : (2 * pair + 2) * inputs]
                parts = (
                    jnp.where(low, even, pltpu.roll(odd, quarter, 1)),
                    jnp.where(low, pltpu.roll(even, wide - quarter, 1), odd),
                )
                for core, part in enumerate(parts):
                    row = (2 * f + core) * inputs
                    at = (slice(row, row + inputs), slice(pair * wide, (pair + 1) * wide))
                    z_ref[at] = part.astype(jnp.bfloat16)
                    w_ref[at] = (pltpu.roll(part, wide // 2, 1) * sign).astype(jnp.bfloat16)
        every = z_ref[...]
        for part, left in enumerate((z_ref, w_ref)):
            sums = lax.dot_general(
                left[...], every, (((1,), (1,)), ((), ())), preferred_element_type=jnp.float32
            )
            sums = (sums * scale).astype(jnp.bfloat16)
            for f in range(feeds):
                out[f, part, k] = sums[2 * f * inputs : 2 * (f + 1) * inputs]


def correlate(received, feeds, inputs, scale):
    channels, rows, lanes = received.shape
    total = feeds * 2 * inputs
    depth = rows * lanes // total
    return pl.pallas_call(
        functools.partial(correlate_kernel, feeds, inputs, scale),
        out_shape=jax.ShapeDtypeStruct((feeds, 2, channels, 2 * inputs, total), jnp.bfloat16),
        scratch_shapes=[pltpu.VMEM((total, depth), jnp.bfloat16)] * 2,
        compiler_params=pltpu.CompilerParams(vmem_limit_bytes=32 * 2**20),
    )(received)


def body(table, voltages, previous, filter_taps):
    inputs, block = voltages.shape
    feeds, times = lax.axis_size("feed"), lax.axis_size("tm")
    chips = times // CORES
    here = inputs // CORES
    place = lax.axis_index("tm").astype(jnp.int32)
    chip, core = place // CORES, place % CORES
    own = lax.all_to_all(
        voltages.reshape(CORES, here, block), "tm", 0, 0,
        axis_index_groups=[[c * CORES + o for o in range(CORES)] for c in range(chips)], tiled=True,
    )
    ups = [(t, t + CORES) for t in range(times - CORES)]
    downs = [(t, (t - CORES) % times) for t in range(times)]
    right = lax.ppermute(own, "tm", downs)
    left = lax.ppermute(own, "tm", ups)
    numbers = jnp.stack([chip, jnp.int32(chips), core * here])
    spectra = channelize(numbers, left, own, right, previous, filter_taps, table)
    rows = spectra.shape[1]
    per_device = HALF // (feeds * times)
    received = lax.all_to_all(
        spectra.reshape(feeds * times, per_device * 2, rows), ("feed", "tm"), 0, 0, tiled=True
    )
    received = received.reshape(feeds, chips, CORES, per_device, 2, rows).transpose(3, 0, 4, 2, 1, 5)
    received = received.reshape(per_device, feeds * 2 * times, rows)
    result = correlate(received, feeds, here, FRAME / (times * block))
    result = lax.all_to_all(result, "feed", 0, 0, tiled=True)
    result = result.transpose(1, 0, 2, 3, 4).astype(jnp.float32)
    return result.reshape(2, feeds * per_device, inputs, feeds * inputs)


def solution(mesh):
    sizes = dict(mesh.shape)
    table = dft_table(sizes["feed"], sizes["tm"])
    placed = (P("feed", "tm"), P("feed", None), P())

    def run(voltages, previous, filter_taps):
        return jax.shard_map(
            functools.partial(body, jnp.asarray(table)),
            mesh=mesh,
            in_specs=placed,
            out_specs=P(None, "tm", "feed", None),
            check_vma=False,
        )(voltages, previous, filter_taps)

    return run
```

```python
import functools
import math

import jax
import jax.numpy as jnp
import ml_dtypes
import numpy as np
from jax import lax
from jax.experimental import pallas as pl
from jax.experimental.pallas import tpu as pltpu
from jax.sharding import Mesh
from jax.sharding import PartitionSpec as P

FRAME = 2048
HALF = FRAME // 2
TAPS = 16
REACH = TAPS - 1
STEPS = 2
CORES = 2
VMEM_BYTES = 20 * 2**20
LOAD_BYTES = 12 * 2**20


AXES = {"y": 4, "half": 2, "x": 4, "z": 8, "core": 2}
FEED = ("y", "half")
TIME = ("x", "z", "core")
CHIP = ("x", "z")
ORDER = ("core", "x", "y", "z", "half")
PAIR = 2
BLOCK = AXES["z"] * AXES["half"] * PAIR * 2


def dft_table():
    parity = np.arange(2).reshape(2, 1, 1, 1, 1, 1, 1)
    core = np.arange(2).reshape(1, 2, 1, 1, 1, 1, 1)
    x = np.arange(4).reshape(1, 1, 4, 1, 1, 1, 1)
    upper = np.arange(2).reshape(1, 1, 1, 2, 1, 1, 1)
    z = np.arange(8).reshape(1, 1, 1, 1, 8, 1, 1)
    half = np.arange(2).reshape(1, 1, 1, 1, 1, 2, 1)
    pair = np.arange(PAIR).reshape(1, 1, 1, 1, 1, 1, PAIR)
    time = (x * 8 + z) * 2 + core
    channel = time * 16 + pair * 8 + upper * 4 + half * 2 + parity
    turns = (channel.reshape(-1, 1) * np.arange(FRAME // 2)[None, :]) % FRAME
    angle = turns * (2.0 * math.pi / FRAME)
    table = np.stack([np.cos(angle), -np.sin(angle)], axis=1)
    return table.reshape(2, HALF, FRAME // 2).astype(ml_dtypes.bfloat16)


def load_kernel(first_ref, table, previous, table_here, previous_here, arrived):
    inputs = previous_here.shape[0]
    rows = pl.ds(pl.multiple_of(first_ref[0], inputs), inputs)
    copies = (
        pltpu.make_async_copy(table, table_here, arrived.at[0]),
        pltpu.make_async_copy(previous.at[rows], previous_here, arrived.at[1]),
    )
    for copy in copies:
        copy.start()
    for copy in copies:
        copy.wait()


def load(first, table, previous, inputs):
    on_chip = pl.BlockSpec(memory_space=pltpu.VMEM)
    return pl.pallas_call(
        load_kernel,
        out_shape=(
            jax.ShapeDtypeStruct(table.shape, table.dtype),
            jax.ShapeDtypeStruct((inputs, previous.shape[1]), previous.dtype),
        ),
        in_specs=[pl.BlockSpec(memory_space=pltpu.SMEM)] + [pl.BlockSpec(memory_space=pl.ANY)] * 2,
        out_specs=(on_chip, on_chip),
        scratch_shapes=[pltpu.SemaphoreType.DMA((2,))],
        compiler_params=pltpu.CompilerParams(vmem_limit_bytes=LOAD_BYTES),
    )(first, table, previous)


def channelize_kernel(place_ref, left, own, right, previous, taps, table, out, folded):
    cores, inputs, block = own.shape
    here = block // FRAME
    spectra = cores * here
    back = REACH - spectra
    chip = place_ref[0]
    at_start = chip == 0
    at_end = chip == place_ref[1] - 1

    def columns(j, carry):
        parts = []
        for part in range(2):
            lane = pl.multiple_of(part * (FRAME // 2) + j * 128, 128)
            weights = [taps[t : t + 1, pl.ds(lane, 128)] for t in range(TAPS)]
            frames = []
            for w in range(spectra + REACH):
                source = (left, own, right)[(w + spectra - back) // spectra]
                frame = (w + spectra - back) % spectra
                at = pl.ds(pl.multiple_of(frame % here * FRAME + lane, 128), 128)
                value = source[frame // here, :, at].astype(jnp.float32)
                if w < REACH:
                    held = w if w >= back else jnp.where(at_start, w + spectra, w)
                    at = pl.ds(pl.multiple_of(held * FRAME + lane, 128), 128)
                    old = previous[:, at].astype(jnp.float32)
                    use_old = at_end if w >= back else jnp.logical_or(at_start, at_end)
                    value = jnp.where(use_old, old, value)
                frames.append(value)
            totals = []
            for s in range(spectra):
                total = weights[0] * frames[s]
                for t in range(1, TAPS):
                    total = total + weights[t] * frames[s + t]
                totals.append(total)
            parts.append(totals)
        at = pl.ds(pl.multiple_of(j * 128, 128), 128)
        for s, (low, high) in enumerate(zip(*parts)):
            rows = pl.ds(s * inputs, inputs)
            folded[0, rows, at] = (low + high).astype(jnp.bfloat16)
            folded[1, rows, at] = (low - high).astype(jnp.bfloat16)
        return carry

    lax.fori_loop(0, FRAME // 2 // 128, columns, 0)
    step = table.shape[1] // STEPS
    for parity in range(2):
        for j in range(STEPS):
            spectrum = lax.dot_general(
                table[parity, j * step : (j + 1) * step, :],
                folded[parity],
                (((1,), (1,)), ((), ())),
                preferred_element_type=jnp.float32,
            )
            spectrum = (spectrum * (1.0 / math.sqrt(FRAME))).astype(jnp.bfloat16)
            for block in range(step // BLOCK):
                row = ((j * (step // BLOCK) + block) * 2 + parity) * BLOCK
                out[row : row + BLOCK, :] = spectrum[block * BLOCK : (block + 1) * BLOCK]


def channelize(place, left, own, right, previous, taps, table):
    cores, inputs, block = own.shape
    rows = cores * inputs * (block // FRAME)
    on_chip = pl.BlockSpec(memory_space=pltpu.VMEM)
    return pl.pallas_call(
        channelize_kernel,
        out_shape=jax.ShapeDtypeStruct((2 * table.shape[1], rows), jnp.bfloat16),
        in_specs=[pl.BlockSpec(memory_space=pltpu.SMEM)] + [on_chip] * 6,
        out_specs=on_chip,
        scratch_shapes=[pltpu.VMEM((2, rows, FRAME // 2), jnp.bfloat16)],
        compiler_params=pltpu.CompilerParams(vmem_limit_bytes=VMEM_BYTES),
    )(place, left, own, right, previous, taps, table)


def correlate_kernel(feeds, inputs, scale, received, out, both):
    channels, rows, lanes = received.shape
    wide = rows // feeds
    quarter = wide // 4
    total = both.shape[1] // 2
    lane = lax.broadcasted_iota(jnp.int32, (inputs, wide), 1)
    sign = jnp.where(lane < wide // 2, 1.0, -1.0)
    low = lane % (2 * quarter) < quarter
    for k in range(channels):
        for f in range(feeds):
            turned = received[k, f * wide : (f + 1) * wide, :].T.astype(jnp.float32)
            for pair in range(lanes // inputs // 2):
                even = turned[2 * pair * inputs : (2 * pair + 1) * inputs]
                odd = turned[(2 * pair + 1) * inputs : (2 * pair + 2) * inputs]
                parts = (
                    jnp.where(low, even, pltpu.roll(odd, quarter, 1)),
                    jnp.where(low, pltpu.roll(even, wide - quarter, 1), odd),
                )
                for core, part in enumerate(parts):
                    row = (2 * f + core) * inputs
                    at = slice(pair * wide, (pair + 1) * wide)
                    both[k, row : row + inputs, at] = part.astype(jnp.bfloat16)
                    part = pltpu.roll(part, wide // 2, 1) * sign
                    both[k, total + row : total + row + inputs, at] = part.astype(jnp.bfloat16)
    for k in range(channels):
        sums = lax.dot_general(
            both[k], both[k, :total], (((1,), (1,)), ((), ())), preferred_element_type=jnp.float32
        )
        sums = (sums * scale).astype(jnp.bfloat16)
        for part in range(2):
            for f in range(feeds):
                row = part * total + 2 * f * inputs
                out[f, part, k] = sums[row : row + 2 * inputs]


def correlate(received, feeds, inputs, scale):
    channels, rows, lanes = received.shape
    total = feeds * 2 * inputs
    depth = rows * lanes // total
    return pl.pallas_call(
        functools.partial(correlate_kernel, feeds, inputs, scale),
        out_shape=jax.ShapeDtypeStruct((feeds, 2, channels, 2 * inputs, total), jnp.bfloat16),
        scratch_shapes=[pltpu.VMEM((channels, 2 * total, depth), jnp.bfloat16)],
        compiler_params=pltpu.CompilerParams(vmem_limit_bytes=32 * 2**20),
    )(received)


def body(table, voltages, previous, filter_taps):
    inputs, block = voltages.shape
    feeds, chips = math.prod(AXES[a] for a in FEED), math.prod(AXES[a] for a in CHIP)
    here = inputs // CORES
    chip, core = lax.axis_index(CHIP), lax.axis_index("core")
    own = lax.all_to_all(voltages.reshape(CORES, here, block), "core", 0, 0, tiled=True)
    right = lax.ppermute(own, CHIP, [(c, (c - 1) % chips) for c in range(chips)])
    left = lax.ppermute(own, CHIP, [(c, c + 1) for c in range(chips - 1)])
    first = (core * here).astype(jnp.int32).reshape(1)
    table, old = load(first, table, previous, here)
    numbers = jnp.stack([chip.astype(jnp.int32), jnp.int32(chips)])
    spectra = channelize(numbers, left, own, right, old, filter_taps, table)
    rows = spectra.shape[1]
    devices = math.prod(AXES.values())
    received = lax.all_to_all(spectra.reshape(devices, PAIR * 2, rows), ORDER, 0, 0, tiled=True)
    received = received.reshape(*(AXES[a] for a in ORDER), PAIR, 2, rows)
    received = received.transpose(5, 2, 4, 6, 0, 1, 3, 7).reshape(PAIR, -1, rows)
    result = correlate(received, feeds, here, FRAME / (chips * CORES * block))
    result = lax.all_to_all(result, FEED, 0, 0, tiled=True)
    result = result.reshape(2, 2, 2, 2, PAIR, inputs, feeds * inputs).transpose(3, 4, 0, 2, 1, 5, 6)
    return result.astype(jnp.float32).reshape(2, feeds * PAIR, inputs, feeds * inputs)


def solution(mesh):
    parts = Mesh(mesh.devices.reshape(tuple(AXES.values())), tuple(AXES))
    table = dft_table()
    placed = (P(FEED, TIME), P(FEED, None), P())

    def run(voltages, previous, filter_taps):
        return jax.shard_map(
            functools.partial(body, jnp.asarray(table)),
            mesh=parts,
            in_specs=placed,
            out_specs=P(None, TIME, FEED, None),
            check_vma=False,
        )(voltages, previous, filter_taps)

    return run
```

```python
import functools
import math

import jax
import jax.numpy as jnp
import ml_dtypes
import numpy as np
from jax import lax
from jax.experimental import pallas as pl
from jax.experimental.pallas import tpu as pltpu
from jax.sharding import Mesh
from jax.sharding import PartitionSpec as P

FRAME = 2048
HALF = FRAME // 2
TAPS = 16
REACH = TAPS - 1
STEPS = 2
CORES = 2
VMEM_BYTES = 20 * 2**20
LOAD_BYTES = 12 * 2**20


AXES = {"y": 4, "half": 2, "x": 4, "z": 8, "core": 2}
FEED = ("y", "half")
TIME = ("x", "z", "core")
CHIP = ("x", "z")
ORDER = ("half", "core", "x", "y", "z")
CHANNELS = 4
BLOCK = AXES["z"] * CHANNELS * 2


def dft_table():
    parity = np.arange(2).reshape(2, 1, 1, 1, 1, 1)
    core = np.arange(2).reshape(1, 2, 1, 1, 1, 1)
    x = np.arange(4).reshape(1, 1, 4, 1, 1, 1)
    upper = np.arange(2).reshape(1, 1, 1, 2, 1, 1)
    z = np.arange(8).reshape(1, 1, 1, 1, 8, 1)
    own = np.arange(CHANNELS).reshape(1, 1, 1, 1, 1, CHANNELS)
    channel = ((x * 8 + z) * 2 + core) * 16 + own * 4 + upper * 2 + parity
    turns = (channel.reshape(-1, 1) * np.arange(FRAME // 2)[None, :]) % FRAME
    angle = turns * (2.0 * math.pi / FRAME)
    table = np.stack([np.cos(angle), -np.sin(angle)], axis=1)
    return table.reshape(2, HALF, FRAME // 2).astype(ml_dtypes.bfloat16)


def load_kernel(first_ref, table, previous, table_here, previous_here, arrived):
    inputs = previous_here.shape[0]
    rows = pl.ds(pl.multiple_of(first_ref[0], inputs), inputs)
    copies = (
        pltpu.make_async_copy(table, table_here, arrived.at[0]),
        pltpu.make_async_copy(previous.at[rows], previous_here, arrived.at[1]),
    )
    for copy in copies:
        copy.start()
    for copy in copies:
        copy.wait()


def load(first, table, previous, inputs):
    on_chip = pl.BlockSpec(memory_space=pltpu.VMEM)
    return pl.pallas_call(
        load_kernel,
        out_shape=(
            jax.ShapeDtypeStruct(table.shape, table.dtype),
            jax.ShapeDtypeStruct((inputs, previous.shape[1]), previous.dtype),
        ),
        in_specs=[pl.BlockSpec(memory_space=pltpu.SMEM)] + [pl.BlockSpec(memory_space=pl.ANY)] * 2,
        out_specs=(on_chip, on_chip),
        scratch_shapes=[pltpu.SemaphoreType.DMA((2,))],
        compiler_params=pltpu.CompilerParams(vmem_limit_bytes=LOAD_BYTES),
    )(first, table, previous)


def channelize_kernel(place_ref, left, own, right, previous, taps, table, out, folded):
    cores, inputs, block = own.shape
    here = block // FRAME
    spectra = cores * here
    back = REACH - spectra
    chip = place_ref[0]
    at_start = chip == 0
    at_end = chip == place_ref[1] - 1

    def columns(j, carry):
        parts = []
        for part in range(2):
            lane = pl.multiple_of(part * (FRAME // 2) + j * 128, 128)
            weights = [taps[t : t + 1, pl.ds(lane, 128)] for t in range(TAPS)]
            frames = []
            for w in range(spectra + REACH):
                source = (left, own, right)[(w + spectra - back) // spectra]
                frame = (w + spectra - back) % spectra
                at = pl.ds(pl.multiple_of(frame % here * FRAME + lane, 128), 128)
                value = source[frame // here, :, at].astype(jnp.float32)
                if w < REACH:
                    held = w if w >= back else jnp.where(at_start, w + spectra, w)
                    at = pl.ds(pl.multiple_of(held * FRAME + lane, 128), 128)
                    old = previous[:, at].astype(jnp.float32)
                    use_old = at_end if w >= back else jnp.logical_or(at_start, at_end)
                    value = jnp.where(use_old, old, value)
                frames.append(value)
            totals = []
            for s in range(spectra):
                total = weights[0] * frames[s]
                for t in range(1, TAPS):
                    total = total + weights[t] * frames[s + t]
                totals.append(total)
            parts.append(totals)
        at = pl.ds(pl.multiple_of(j * 128, 128), 128)
        for s, (low, high) in enumerate(zip(*parts)):
            rows = pl.ds(s * inputs, inputs)
            folded[0, rows, at] = (low + high).astype(jnp.bfloat16)
            folded[1, rows, at] = (low - high).astype(jnp.bfloat16)
        return carry

    lax.fori_loop(0, FRAME // 2 // 128, columns, 0)
    step = table.shape[1] // STEPS
    for parity in range(2):
        for j in range(STEPS):
            spectrum = lax.dot_general(
                table[parity, j * step : (j + 1) * step, :],
                folded[parity],
                (((1,), (1,)), ((), ())),
                preferred_element_type=jnp.float32,
            )
            spectrum = (spectrum * (1.0 / math.sqrt(FRAME))).astype(jnp.bfloat16)
            for block in range(step // BLOCK):
                row = ((j * (step // BLOCK) + block) * 2 + parity) * BLOCK
                for half in range(out.shape[0]):
                    out[half, row : row + BLOCK, :] = spectrum[block * BLOCK : (block + 1) * BLOCK]


def channelize(place, left, own, right, previous, taps, table):
    cores, inputs, block = own.shape
    rows = cores * inputs * (block // FRAME)
    on_chip = pl.BlockSpec(memory_space=pltpu.VMEM)
    return pl.pallas_call(
        channelize_kernel,
        out_shape=jax.ShapeDtypeStruct((AXES["half"], 2 * table.shape[1], rows), jnp.bfloat16),
        in_specs=[pl.BlockSpec(memory_space=pltpu.SMEM)] + [on_chip] * 6,
        out_specs=on_chip,
        scratch_shapes=[pltpu.VMEM((2, rows, FRAME // 2), jnp.bfloat16)],
        compiler_params=pltpu.CompilerParams(vmem_limit_bytes=VMEM_BYTES),
    )(place, left, own, right, previous, taps, table)


def correlate_kernel(inputs, scale, place_ref, received, out, every, own):
    channels, rows, lanes = received.shape
    halves, count = AXES["half"], AXES["y"]
    wide = rows // (halves * count)
    quarter = wide // 4
    block = 2 * inputs
    lane = lax.broadcasted_iota(jnp.int32, (inputs, wide), 1)
    low = lane % (2 * quarter) < quarter
    sign = jnp.where(lax.broadcasted_iota(jnp.int32, (block, wide), 1) < wide // 2, 1.0, -1.0)
    for k in range(channels):
        for half in range(halves):
            for y in range(count):
                first = (half * count + y) * wide
                turned = received[k, first : first + wide, :].T.astype(jnp.float32)
                for pair in range(lanes // inputs // 2):
                    even = turned[2 * pair * inputs : (2 * pair + 1) * inputs]
                    odd = turned[(2 * pair + 1) * inputs : (2 * pair + 2) * inputs]
                    parts = (
                        jnp.where(low, even, pltpu.roll(odd, quarter, 1)),
                        jnp.where(low, pltpu.roll(even, wide - quarter, 1), odd),
                    )
                    for core, part in enumerate(parts):
                        row = (y * halves + half) * block + core * inputs
                        at = slice(pair * wide, (pair + 1) * wide)
                        every[k, row : row + inputs, at] = part.astype(jnp.bfloat16)
        for y in range(count):
            row = pl.multiple_of((y * halves + place_ref[2]) * block, block)
            for pair in range(lanes // inputs // 2):
                at = slice(pair * wide, (pair + 1) * wide)
                part = every[k, pl.ds(row, block), at]
                own[k, y * block : (y + 1) * block, at] = part
                part = pltpu.roll(part.astype(jnp.float32), wide // 2, 1) * sign
                own[k, (count + y) * block : (count + y + 1) * block, at] = part.astype(jnp.bfloat16)
    for k in range(channels):
        sums = lax.dot_general(
            own[k], every[k], (((1,), (1,)), ((), ())), preferred_element_type=jnp.float32
        )
        sums = (sums * scale).astype(jnp.bfloat16)
        for part in range(2):
            for y in range(count):
                row = (part * count + y) * block
                out[y, part, k] = sums[row : row + block]


def correlate(place, received, inputs, scale):
    channels, rows, lanes = received.shape
    count, total = AXES["y"], AXES["y"] * AXES["half"] * 2 * inputs
    depth = rows * lanes // total
    return pl.pallas_call(
        functools.partial(correlate_kernel, inputs, scale),
        out_shape=jax.ShapeDtypeStruct((count, 2, channels, 2 * inputs, total), jnp.bfloat16),
        in_specs=[pl.BlockSpec(memory_space=pltpu.SMEM), pl.BlockSpec(memory_space=pltpu.VMEM)],
        out_specs=pl.BlockSpec(memory_space=pltpu.VMEM),
        scratch_shapes=[pltpu.VMEM((channels, total, depth), jnp.bfloat16)] * 2,
        compiler_params=pltpu.CompilerParams(vmem_limit_bytes=32 * 2**20),
    )(place, received)


def body(table, voltages, previous, filter_taps):
    inputs, block = voltages.shape
    feeds, chips = math.prod(AXES[a] for a in FEED), math.prod(AXES[a] for a in CHIP)
    here = inputs // CORES
    chip, core = lax.axis_index(CHIP), lax.axis_index("core")
    own = lax.all_to_all(voltages.reshape(CORES, here, block), "core", 0, 0, tiled=True)
    right = lax.ppermute(own, CHIP, [(c, (c - 1) % chips) for c in range(chips)])
    left = lax.ppermute(own, CHIP, [(c, c + 1) for c in range(chips - 1)])
    first = (core * here).astype(jnp.int32).reshape(1)
    table, old = load(first, table, previous, here)
    numbers = jnp.stack([chip.astype(jnp.int32), jnp.int32(chips), lax.axis_index("half").astype(jnp.int32)])
    spectra = channelize(numbers, left, own, right, old, filter_taps, table)
    rows = spectra.shape[2]
    devices = math.prod(AXES.values())
    received = lax.all_to_all(spectra.reshape(devices, CHANNELS * 2, rows), ORDER, 0, 0, tiled=True)
    received = received.reshape(*(AXES[a] for a in ORDER), CHANNELS, 2, rows)
    received = received.transpose(5, 0, 3, 6, 1, 2, 4, 7).reshape(CHANNELS, -1, rows)
    result = correlate(numbers, received, here, FRAME / (chips * CORES * block))
    result = lax.all_to_all(result, "y", 0, 0, tiled=True)
    result = result.transpose(1, 2, 0, 3, 4).astype(jnp.float32)
    return result.reshape(2, AXES["y"] * CHANNELS, inputs, feeds * inputs)


def solution(mesh):
    parts = Mesh(mesh.devices.reshape(tuple(AXES.values())), tuple(AXES))
    table = dft_table()
    placed = (P(FEED, TIME), P(FEED, None), P())

    def run(voltages, previous, filter_taps):
        return jax.shard_map(
            functools.partial(body, jnp.asarray(table)),
            mesh=parts,
            in_specs=placed,
            out_specs=P(None, TIME, FEED, None),
            check_vma=False,
        )(voltages, previous, filter_taps)

    return run
```

```python
import functools
import math

import jax
import jax.numpy as jnp
import ml_dtypes
import numpy as np
from jax import lax
from jax.experimental import pallas as pl
from jax.experimental.pallas import tpu as pltpu
from jax.sharding import Mesh
from jax.sharding import PartitionSpec as P

FRAME = 2048
HALF = FRAME // 2
TAPS = 16
REACH = TAPS - 1
AHEAD = 8
STEPS = 2
VMEM_BYTES = 20 * 2**20
LOAD_BYTES = 12 * 2**20


AXES = {"y": 4, "half": 2, "x": 4, "z": 8, "core": 2}
FEED = ("y", "half")
TIME = ("x", "z", "core")
CHIP = ("x", "z")
ORDER = ("half", "core", "x", "y", "z")
CHANNELS = 4
BLOCK = AXES["z"] * CHANNELS * 2


def dft_table():
    parity = np.arange(2).reshape(2, 1, 1, 1, 1, 1)
    core = np.arange(2).reshape(1, 2, 1, 1, 1, 1)
    x = np.arange(4).reshape(1, 1, 4, 1, 1, 1)
    upper = np.arange(2).reshape(1, 1, 1, 2, 1, 1)
    z = np.arange(8).reshape(1, 1, 1, 1, 8, 1)
    own = np.arange(CHANNELS).reshape(1, 1, 1, 1, 1, CHANNELS)
    channel = ((x * 8 + z) * 2 + core) * 16 + own * 4 + upper * 2 + parity
    turns = (channel.reshape(-1, 1) * np.arange(FRAME // 2)[None, :]) % FRAME
    angle = turns * (2.0 * math.pi / FRAME)
    table = np.stack([np.cos(angle), -np.sin(angle)], axis=1)
    return table.reshape(2, HALF, FRAME // 2).astype(ml_dtypes.bfloat16)


def load_kernel(table, previous, table_here, previous_here, arrived):
    copies = (
        pltpu.make_async_copy(table, table_here, arrived.at[0]),
        pltpu.make_async_copy(previous, previous_here, arrived.at[1]),
    )
    for copy in copies:
        copy.start()
    for copy in copies:
        copy.wait()


def load(table, previous):
    on_chip = pl.BlockSpec(memory_space=pltpu.VMEM)
    return pl.pallas_call(
        load_kernel,
        out_shape=tuple(jax.ShapeDtypeStruct(a.shape, a.dtype) for a in (table, previous)),
        in_specs=[pl.BlockSpec(memory_space=pl.ANY)] * 2,
        out_specs=(on_chip, on_chip),
        scratch_shapes=[pltpu.SemaphoreType.DMA((2,))],
        compiler_params=pltpu.CompilerParams(vmem_limit_bytes=LOAD_BYTES),
    )(table, previous)


def channelize_kernel(place_ref, own, swapped, first, passed, second, previous, taps, table, out, folded):
    inputs, block = own.shape
    here = block // FRAME
    start = place_ref[0]

    def filter_frames(sources):
        def columns(j, carry):
            for row in range(0, inputs, 16):
                parts = []
                for part in range(2):
                    lane = pl.multiple_of(part * (FRAME // 2) + j * 128, 128)
                    weights = [taps[t : t + 1, pl.ds(lane, 128)] for t in range(TAPS)]
                    frames = []
                    for w in range(here + REACH):
                        source, frame = sources[(w + 1) // here], (w + 1) % here
                        at = pl.ds(pl.multiple_of(frame * FRAME + lane, 128), 128)
                        value = source[row : row + 16, at].astype(jnp.float32)
                        if w < REACH:
                            held = jnp.clip(start + w + REACH, 0, REACH - 1) * FRAME + lane
                            at = pl.ds(pl.multiple_of(held, 128), 128)
                            old = previous[row : row + 16, at].astype(jnp.float32)
                            value = jnp.where(start + w < 0, old, value)
                        frames.append(value)
                    totals = []
                    for s in range(here):
                        total = weights[0] * frames[s]
                        for t in range(1, TAPS):
                            total = total + weights[t] * frames[s + t]
                        totals.append(total)
                    parts.append(totals)
                at = pl.ds(pl.multiple_of(j * 128, 128), 128)
                for s, (low, high) in enumerate(zip(*parts)):
                    rows = pl.ds(s * inputs + row, 16)
                    folded[0, rows, at] = (low + high).astype(jnp.bfloat16)
                    folded[1, rows, at] = (low - high).astype(jnp.bfloat16)
            return carry

        lax.fori_loop(0, FRAME // 2 // 128, columns, 0)

    @pl.when(place_ref[1] == 0)
    def _():
        filter_frames((second, passed, own, swapped, first))

    @pl.when(place_ref[1] == 1)
    def _():
        filter_frames((first, swapped, own, passed, second))

    step = table.shape[1] // STEPS
    for parity in range(2):
        for j in range(STEPS):
            spectrum = lax.dot_general(
                table[parity, j * step : (j + 1) * step, :],
                folded[parity],
                (((1,), (1,)), ((), ())),
                preferred_element_type=jnp.float32,
            )
            spectrum = (spectrum * (1.0 / math.sqrt(FRAME))).astype(jnp.bfloat16)
            for block in range(step // BLOCK):
                row = ((j * (step // BLOCK) + block) * 2 + parity) * BLOCK
                for half in range(out.shape[0]):
                    out[half, row : row + BLOCK, :] = spectrum[block * BLOCK : (block + 1) * BLOCK]


def channelize(place, blocks, previous, taps, table):
    inputs, block = blocks[0].shape
    rows = inputs * (block // FRAME)
    on_chip = pl.BlockSpec(memory_space=pltpu.VMEM)
    operands = (*blocks, previous, taps, table)
    return pl.pallas_call(
        channelize_kernel,
        out_shape=jax.ShapeDtypeStruct((AXES["half"], 2 * table.shape[1], rows), jnp.bfloat16),
        in_specs=[pl.BlockSpec(memory_space=pltpu.SMEM)] + [on_chip] * len(operands),
        out_specs=on_chip,
        scratch_shapes=[pltpu.VMEM((2, rows, FRAME // 2), jnp.bfloat16)],
        compiler_params=pltpu.CompilerParams(vmem_limit_bytes=VMEM_BYTES),
    )(place, *operands)


def correlate_kernel(inputs, scale, place_ref, received, out, every, own):
    channels, rows, lanes = received.shape
    halves, count = AXES["half"], AXES["y"]
    wide = rows // (halves * count)
    sign = jnp.where(lax.broadcasted_iota(jnp.int32, (inputs, wide), 1) < wide // 2, 1.0, -1.0)
    for k in range(channels):
        for half in range(halves):
            for y in range(count):
                first = (half * count + y) * wide
                turned = received[k, first : first + wide, :].T
                row = (y * halves + half) * inputs
                for s in range(lanes // inputs):
                    at = slice(s * wide, (s + 1) * wide)
                    every[k, row : row + inputs, at] = turned[s * inputs : (s + 1) * inputs]
        for y in range(count):
            row = pl.multiple_of((y * halves + place_ref[2]) * inputs, inputs)
            for s in range(lanes // inputs):
                at = slice(s * wide, (s + 1) * wide)
                part = every[k, pl.ds(row, inputs), at]
                own[k, y * inputs : (y + 1) * inputs, at] = part
                part = pltpu.roll(part.astype(jnp.float32), wide // 2, 1) * sign
                own[k, (count + y) * inputs : (count + y + 1) * inputs, at] = part.astype(jnp.bfloat16)
    for k in range(channels):
        sums = lax.dot_general(
            own[k], every[k], (((1,), (1,)), ((), ())), preferred_element_type=jnp.float32
        )
        sums = (sums * scale).astype(jnp.bfloat16)
        for part in range(2):
            for y in range(count):
                row = (part * count + y) * inputs
                out[y, part, k] = sums[row : row + inputs]


def correlate(place, received, inputs, scale):
    channels, rows, lanes = received.shape
    count, total = AXES["y"], AXES["y"] * AXES["half"] * inputs
    depth = rows * lanes // total
    return pl.pallas_call(
        functools.partial(correlate_kernel, inputs, scale),
        out_shape=jax.ShapeDtypeStruct((count, 2, channels, inputs, total), jnp.bfloat16),
        in_specs=[pl.BlockSpec(memory_space=pltpu.SMEM), pl.BlockSpec(memory_space=pltpu.VMEM)],
        out_specs=pl.BlockSpec(memory_space=pltpu.VMEM),
        scratch_shapes=[pltpu.VMEM((channels, total, depth), jnp.bfloat16)] * 2,
        compiler_params=pltpu.CompilerParams(vmem_limit_bytes=32 * 2**20),
    )(place, received)


def widen_kernel(result, out, wide, sent):
    count, parts, channels = result.shape[:3]
    copies = []
    for part in range(parts):
        for k in range(channels):
            for y in range(count):
                wide[part, k * count + y] = result[y, part, k].astype(jnp.float32)
            at = pl.ds(k * count, count)
            copy = pltpu.make_async_copy(wide.at[part, at], out.at[part, at], sent.at[part * channels + k])
            copy.start()
            copies.append(copy)
    for copy in copies:
        copy.wait()


def widen(result):
    count, parts, channels, inputs, total = result.shape
    shape = (parts, channels * count, inputs, total)
    return pl.pallas_call(
        widen_kernel,
        out_shape=jax.ShapeDtypeStruct(shape, jnp.float32),
        in_specs=[pl.BlockSpec(memory_space=pltpu.VMEM)],
        out_specs=pl.BlockSpec(memory_space=pl.ANY),
        scratch_shapes=[pltpu.VMEM(shape, jnp.float32), pltpu.SemaphoreType.DMA((parts * channels,))],
        compiler_params=pltpu.CompilerParams(vmem_limit_bytes=16 * 2**20),
    )(result)


def body(table, voltages, previous, filter_taps):
    inputs, block = voltages.shape
    here = block // FRAME
    chips, cores = math.prod(AXES[a] for a in CHIP), AXES["core"]
    chip, core = lax.axis_index(CHIP), lax.axis_index("core")
    up = [(c, c + 1) for c in range(chips - 2)]
    down = [(c, (c - 1) % chips) for c in range(chips)]
    route = lambda steps, core: [(a * cores + core, b * cores + core) for a, b in steps]
    first = lax.ppermute(voltages, TIME, route(up, 1) + route(down, 0))
    second = lax.ppermute(voltages, TIME, route(up, 0) + route(down, 1))
    swapped = lax.ppermute(voltages, "core", [(0, 1), (1, 0)])
    passed = lax.ppermute(first, "core", [(0, 1), (1, 0)])
    table, old = load(table, previous)
    start = (chip * cores + core) * here + AHEAD - REACH - jnp.where(chip == chips - 1, chips * cores * here, 0)
    place = jnp.stack([start, core, lax.axis_index("half")]).astype(jnp.int32)
    spectra = channelize(place, (voltages, swapped, first, passed, second), old, filter_taps, table)
    rows = spectra.shape[2]
    devices = math.prod(AXES.values())
    received = lax.all_to_all(spectra.reshape(devices, CHANNELS * 2, rows), ORDER, 0, 0, tiled=True)
    received = received.reshape(*(AXES[a] for a in ORDER), CHANNELS, 2, rows)
    received = received.transpose(5, 0, 3, 6, 1, 2, 4, 7).reshape(CHANNELS, -1, rows)
    result = correlate(place, received, inputs, FRAME / (chips * cores * block))
    result = lax.all_to_all(result, "y", 0, 0, tiled=True)
    return widen(result)


def solution(mesh):
    parts = Mesh(mesh.devices.reshape(tuple(AXES.values())), tuple(AXES))
    table = dft_table()
    placed = (P(FEED, TIME), P(FEED, None), P())

    def run(voltages, previous, filter_taps):
        return jax.shard_map(
            functools.partial(body, jnp.asarray(table)),
            mesh=parts,
            in_specs=placed,
            out_specs=P(None, TIME, FEED, None),
            check_vma=False,
        )(voltages, previous, filter_taps)

    return run
```

```python
import functools
import math

import jax
import jax.numpy as jnp
import ml_dtypes
import numpy as np
from jax import lax
from jax.experimental import pallas as pl
from jax.experimental.pallas import tpu as pltpu
from jax.sharding import Mesh
from jax.sharding import PartitionSpec as P

FRAME = 2048
HALF = FRAME // 2
TAPS = 16
REACH = TAPS - 1
AHEAD = 8
STEPS = 2
VMEM_BYTES = 20 * 2**20
LOAD_BYTES = 12 * 2**20


AXES = {"y": 4, "half": 2, "x": 4, "z": 8, "core": 2}
FEED = ("y", "half")
TIME = ("x", "z", "core")
CHIP = ("x", "z")
ORDER = ("half", "core", "x", "y", "z")
CHANNELS = 4
BLOCK = AXES["z"] * CHANNELS * 2


def dft_table():
    parity = np.arange(2).reshape(2, 1, 1, 1, 1, 1)
    core = np.arange(2).reshape(1, 2, 1, 1, 1, 1)
    x = np.arange(4).reshape(1, 1, 4, 1, 1, 1)
    upper = np.arange(2).reshape(1, 1, 1, 2, 1, 1)
    z = np.arange(8).reshape(1, 1, 1, 1, 8, 1)
    own = np.arange(CHANNELS).reshape(1, 1, 1, 1, 1, CHANNELS)
    channel = ((x * 8 + z) * 2 + core) * 16 + own * 4 + upper * 2 + parity
    turns = (channel.reshape(-1, 1) * np.arange(FRAME // 2)[None, :]) % FRAME
    angle = turns * (2.0 * math.pi / FRAME)
    table = np.stack([np.cos(angle), -np.sin(angle)], axis=1)
    return table.reshape(2, HALF, FRAME // 2).astype(ml_dtypes.bfloat16)


def load_kernel(table, previous, table_here, previous_here, arrived):
    copies = (
        pltpu.make_async_copy(table, table_here, arrived.at[0]),
        pltpu.make_async_copy(previous, previous_here, arrived.at[1]),
    )
    for copy in copies:
        copy.start()
    for copy in copies:
        copy.wait()


def load(table, previous):
    on_chip = pl.BlockSpec(memory_space=pltpu.VMEM)
    return pl.pallas_call(
        load_kernel,
        out_shape=tuple(jax.ShapeDtypeStruct(a.shape, a.dtype) for a in (table, previous)),
        in_specs=[pl.BlockSpec(memory_space=pl.ANY)] * 2,
        out_specs=(on_chip, on_chip),
        scratch_shapes=[pltpu.SemaphoreType.DMA((2,))],
        compiler_params=pltpu.CompilerParams(vmem_limit_bytes=LOAD_BYTES),
    )(table, previous)


def channelize_kernel(place_ref, own, swapped, first, passed, second, previous, taps, table, out, folded):
    inputs, block = own.shape
    here = block // FRAME
    start = place_ref[0]

    def filter_frames(sources):
        held = [jnp.clip(start + w + REACH, 0, REACH - 1) * FRAME for w in range(REACH)]

        def columns(j, carry):
            for row in range(0, inputs, 16):
                parts = []
                for part in range(2):
                    lane = pl.multiple_of(part * (FRAME // 2) + j * 128, 128)
                    weights = [taps[t : t + 1, pl.ds(lane, 128)] for t in range(TAPS)]
                    frames = []
                    for w in range(here + REACH):
                        source, frame = sources[(w + 1) // here], (w + 1) % here
                        at = pl.ds(pl.multiple_of(frame * FRAME + lane, 128), 128)
                        value = source[row : row + 16, at].astype(jnp.float32)
                        if w < REACH:
                            at = pl.ds(pl.multiple_of(held[w] + lane, 128), 128)
                            old = previous[row : row + 16, at].astype(jnp.float32)
                            value = jnp.where(start + w < 0, old, value)
                        frames.append(value)
                    totals = []
                    for s in range(here):
                        total = weights[0] * frames[s]
                        for t in range(1, TAPS):
                            total = total + weights[t] * frames[s + t]
                        totals.append(total)
                    parts.append(totals)
                at = pl.ds(pl.multiple_of(j * 128, 128), 128)
                for s, (low, high) in enumerate(zip(*parts)):
                    rows = pl.ds(s * inputs + row, 16)
                    folded[0, rows, at] = (low + high).astype(jnp.bfloat16)
                    folded[1, rows, at] = (low - high).astype(jnp.bfloat16)
            return carry

        lax.fori_loop(0, FRAME // 2 // 128, columns, 0)

    @pl.when(place_ref[1] == 0)
    def _():
        filter_frames((second, passed, own, swapped, first))

    @pl.when(place_ref[1] == 1)
    def _():
        filter_frames((first, swapped, own, passed, second))

    step = table.shape[1] // STEPS
    for parity in range(2):
        for j in range(STEPS):
            spectrum = lax.dot_general(
                table[parity, j * step : (j + 1) * step, :],
                folded[parity],
                (((1,), (1,)), ((), ())),
                preferred_element_type=jnp.float32,
            )
            spectrum = (spectrum * (1.0 / math.sqrt(FRAME))).astype(jnp.bfloat16)
            for block in range(step // BLOCK):
                row = ((j * (step // BLOCK) + block) * 2 + parity) * BLOCK
                for half in range(out.shape[0]):
                    out[half, row : row + BLOCK, :] = spectrum[block * BLOCK : (block + 1) * BLOCK]


def channelize(place, blocks, previous, taps, table):
    inputs, block = blocks[0].shape
    rows = inputs * (block // FRAME)
    on_chip = pl.BlockSpec(memory_space=pltpu.VMEM)
    operands = (*blocks, previous, taps, table)
    return pl.pallas_call(
        channelize_kernel,
        out_shape=jax.ShapeDtypeStruct((AXES["half"], 2 * table.shape[1], rows), jnp.bfloat16),
        in_specs=[pl.BlockSpec(memory_space=pltpu.SMEM)] + [on_chip] * len(operands),
        out_specs=on_chip,
        scratch_shapes=[pltpu.VMEM((2, rows, FRAME // 2), jnp.bfloat16)],
        compiler_params=pltpu.CompilerParams(vmem_limit_bytes=VMEM_BYTES),
    )(place, *operands)


def correlate_kernel(inputs, scale, place_ref, received, out, every, own):
    channels, rows, lanes = received.shape
    halves, count = AXES["half"], AXES["y"]
    wide = rows // (halves * count)
    sign = jnp.where(lax.broadcasted_iota(jnp.int32, (inputs, wide), 1) < wide // 2, 1.0, -1.0)
    for k in range(channels):
        for half in range(halves):
            for y in range(count):
                first = (half * count + y) * wide
                turned = received[k, first : first + wide, :].T
                row = (y * halves + half) * inputs
                for s in range(lanes // inputs):
                    at = slice(s * wide, (s + 1) * wide)
                    every[k, row : row + inputs, at] = turned[s * inputs : (s + 1) * inputs]
        for y in range(count):
            row = pl.multiple_of((y * halves + place_ref[2]) * inputs, inputs)
            for s in range(lanes // inputs):
                at = slice(s * wide, (s + 1) * wide)
                part = every[k, pl.ds(row, inputs), at]
                own[k, y * inputs : (y + 1) * inputs, at] = part
                part = pltpu.roll(part.astype(jnp.float32), wide // 2, 1) * sign
                own[k, (count + y) * inputs : (count + y + 1) * inputs, at] = part.astype(jnp.bfloat16)
    for k in range(channels):
        sums = lax.dot_general(
            own[k], every[k], (((1,), (1,)), ((), ())), preferred_element_type=jnp.float32
        )
        sums = (sums * scale).astype(jnp.bfloat16)
        for part in range(2):
            for y in range(count):
                row = (part * count + y) * inputs
                out[y, part, k] = sums[row : row + inputs]


def correlate(place, received, inputs, scale):
    channels, rows, lanes = received.shape
    count, total = AXES["y"], AXES["y"] * AXES["half"] * inputs
    depth = rows * lanes // total
    return pl.pallas_call(
        functools.partial(correlate_kernel, inputs, scale),
        out_shape=jax.ShapeDtypeStruct((count, 2, channels, inputs, total), jnp.bfloat16),
        in_specs=[pl.BlockSpec(memory_space=pltpu.SMEM), pl.BlockSpec(memory_space=pltpu.VMEM)],
        out_specs=pl.BlockSpec(memory_space=pltpu.VMEM),
        scratch_shapes=[pltpu.VMEM((channels, total, depth), jnp.bfloat16)] * 2,
        compiler_params=pltpu.CompilerParams(vmem_limit_bytes=32 * 2**20),
    )(place, received)


def widen_kernel(result, out, wide, sent):
    count, parts, channels = result.shape[:3]
    copies = []
    for part in range(parts):
        for k in range(channels):
            for y in range(count):
                wide[part, k * count + y] = result[y, part, k].astype(jnp.float32)
            at = pl.ds(k * count, count)
            copy = pltpu.make_async_copy(wide.at[part, at], out.at[part, at], sent.at[part * channels + k])
            copy.start()
            copies.append(copy)
    for copy in copies:
        copy.wait()


def widen(result):
    count, parts, channels, inputs, total = result.shape
    shape = (parts, channels * count, inputs, total)
    return pl.pallas_call(
        widen_kernel,
        out_shape=jax.ShapeDtypeStruct(shape, jnp.float32),
        in_specs=[pl.BlockSpec(memory_space=pltpu.VMEM)],
        out_specs=pl.BlockSpec(memory_space=pl.ANY),
        scratch_shapes=[pltpu.VMEM(shape, jnp.float32), pltpu.SemaphoreType.DMA((parts * channels,))],
        compiler_params=pltpu.CompilerParams(vmem_limit_bytes=16 * 2**20),
    )(result)


def body(table, voltages, previous, filter_taps):
    inputs, block = voltages.shape
    here = block // FRAME
    chips, cores = math.prod(AXES[a] for a in CHIP), AXES["core"]
    chip, core = lax.axis_index(CHIP), lax.axis_index("core")
    up = [(c, c + 1) for c in range(chips - 2)]
    down = [(c, (c - 1) % chips) for c in range(chips)]
    route = lambda steps, core: [(a * cores + core, b * cores + core) for a, b in steps]
    first = lax.ppermute(voltages, TIME, route(up, 1) + route(down, 0))
    second = lax.ppermute(voltages, TIME, route(up, 0) + route(down, 1))
    mine, first = lax.optimization_barrier((voltages, first))
    passed = lax.ppermute(first, "core", [(0, 1), (1, 0)])
    swapped = lax.ppermute(mine, "core", [(0, 1), (1, 0)])
    table, old = load(table, previous)
    start = (chip * cores + core) * here + AHEAD - REACH - jnp.where(chip == chips - 1, chips * cores * here, 0)
    place = jnp.stack([start, core, lax.axis_index("half")]).astype(jnp.int32)
    spectra = channelize(place, (voltages, swapped, first, passed, second), old, filter_taps, table)
    rows = spectra.shape[2]
    devices = math.prod(AXES.values())
    received = lax.all_to_all(spectra.reshape(devices, CHANNELS * 2, rows), ORDER, 0, 0, tiled=True)
    received = received.reshape(*(AXES[a] for a in ORDER), CHANNELS, 2, rows)
    received = received.transpose(5, 0, 3, 6, 1, 2, 4, 7).reshape(CHANNELS, -1, rows)
    result = correlate(place, received, inputs, FRAME / (chips * cores * block))
    result = lax.all_to_all(result, "y", 0, 0, tiled=True)
    return widen(result)


def solution(mesh):
    parts = Mesh(mesh.devices.reshape(tuple(AXES.values())), tuple(AXES))
    table = dft_table()
    placed = (P(FEED, TIME), P(FEED, None), P())

    def run(voltages, previous, filter_taps):
        return jax.shard_map(
            functools.partial(body, jnp.asarray(table)),
            mesh=parts,
            in_specs=placed,
            out_specs=P(None, TIME, FEED, None),
            check_vma=False,
        )(voltages, previous, filter_taps)

    return run
```

```python
import functools
import math

import jax
import jax.numpy as jnp
import ml_dtypes
import numpy as np
from jax import lax
from jax.experimental import pallas as pl
from jax.experimental.pallas import tpu as pltpu
from jax.sharding import Mesh
from jax.sharding import PartitionSpec as P

FRAME = 2048
HALF = FRAME // 2
TAPS = 16
REACH = TAPS - 1
AHEAD = 8
STEPS = 2
VMEM_BYTES = 50 * 2**20
LOAD_BYTES = 4 * 2**20


AXES = {"y": 4, "half": 2, "x": 4, "z": 8, "core": 2}
FEED = ("y", "half")
TIME = ("x", "z", "core")
CHIP = ("x", "z")
ORDER = ("half", "core", "x", "y", "z")
CHANNELS = 4
BLOCK = AXES["z"] * CHANNELS * 2


def dft_table():
    parity = np.arange(2).reshape(2, 1, 1, 1, 1, 1)
    core = np.arange(2).reshape(1, 2, 1, 1, 1, 1)
    x = np.arange(4).reshape(1, 1, 4, 1, 1, 1)
    upper = np.arange(2).reshape(1, 1, 1, 2, 1, 1)
    z = np.arange(8).reshape(1, 1, 1, 1, 8, 1)
    own = np.arange(CHANNELS).reshape(1, 1, 1, 1, 1, CHANNELS)
    channel = ((x * 8 + z) * 2 + core) * 16 + own * 4 + upper * 2 + parity
    turns = (channel.reshape(-1, 1) * np.arange(FRAME // 2)[None, :]) % FRAME
    angle = turns * (2.0 * math.pi / FRAME)
    table = np.stack([np.cos(angle), -np.sin(angle)], axis=1)
    return table.reshape(2, HALF, FRAME // 2).astype(ml_dtypes.bfloat16)


def load_kernel(voltages, taps, voltages_here, taps_here, arrived):
    copies = (
        pltpu.make_async_copy(voltages, voltages_here, arrived.at[0]),
        pltpu.make_async_copy(taps, taps_here, arrived.at[1]),
    )
    for copy in copies:
        copy.start()
    for copy in copies:
        copy.wait()


def load(voltages, taps):
    on_chip = pl.BlockSpec(memory_space=pltpu.VMEM)
    return pl.pallas_call(
        load_kernel,
        out_shape=tuple(jax.ShapeDtypeStruct(a.shape, a.dtype) for a in (voltages, taps)),
        in_specs=[pl.BlockSpec(memory_space=pl.ANY)] * 2,
        out_specs=(on_chip, on_chip),
        scratch_shapes=[pltpu.SemaphoreType.DMA((2,))],
        compiler_params=pltpu.CompilerParams(vmem_limit_bytes=LOAD_BYTES),
    )(voltages, taps)


def channelize_kernel(place_ref, own, swapped, first, passed, second, taps, far_previous, far_table, out, folded, previous, table, arrived):
    inputs, block = own.shape
    here = block // FRAME
    start = place_ref[0]
    table_copy = pltpu.make_async_copy(far_table, table, arrived.at[0])
    table_copy.start()

    @pl.when(start < 0)
    def _():
        copy = pltpu.make_async_copy(far_previous, previous, arrived.at[1])
        copy.start()
        copy.wait()

    def filter_frames(sources):
        held = [jnp.clip(start + w + REACH, 0, REACH - 1) * FRAME for w in range(REACH)]

        def columns(j, carry):
            for row in range(0, inputs, 16):
                parts = []
                for part in range(2):
                    lane = pl.multiple_of(part * (FRAME // 2) + j * 128, 128)
                    weights = [taps[t : t + 1, pl.ds(lane, 128)] for t in range(TAPS)]
                    frames = []
                    for w in range(here + REACH):
                        source, frame = sources[(w + 1) // here], (w + 1) % here
                        at = pl.ds(pl.multiple_of(frame * FRAME + lane, 128), 128)
                        value = source[row : row + 16, at].astype(jnp.float32)
                        if w < REACH:
                            at = pl.ds(pl.multiple_of(held[w] + lane, 128), 128)
                            old = previous[row : row + 16, at].astype(jnp.float32)
                            value = jnp.where(start + w < 0, old, value)
                        frames.append(value)
                    totals = []
                    for s in range(here):
                        total = weights[0] * frames[s]
                        for t in range(1, TAPS):
                            total = total + weights[t] * frames[s + t]
                        totals.append(total)
                    parts.append(totals)
                at = pl.ds(pl.multiple_of(j * 128, 128), 128)
                for s, (low, high) in enumerate(zip(*parts)):
                    rows = pl.ds(s * inputs + row, 16)
                    folded[0, rows, at] = (low + high).astype(jnp.bfloat16)
                    folded[1, rows, at] = (low - high).astype(jnp.bfloat16)
            return carry

        lax.fori_loop(0, FRAME // 2 // 128, columns, 0)

    @pl.when(place_ref[1] == 0)
    def _():
        filter_frames((second, passed, own, swapped, first))

    @pl.when(place_ref[1] == 1)
    def _():
        filter_frames((first, swapped, own, passed, second))

    table_copy.wait()
    step = table.shape[1] // STEPS
    for parity in range(2):
        for j in range(STEPS):
            spectrum = lax.dot_general(
                table[parity, j * step : (j + 1) * step, :],
                folded[parity],
                (((1,), (1,)), ((), ())),
                preferred_element_type=jnp.float32,
            )
            spectrum = (spectrum * (1.0 / math.sqrt(FRAME))).astype(jnp.bfloat16)
            for block in range(step // BLOCK):
                row = ((j * (step // BLOCK) + block) * 2 + parity) * BLOCK
                for half in range(out.shape[0]):
                    out[half, row : row + BLOCK, :] = spectrum[block * BLOCK : (block + 1) * BLOCK]


def channelize(place, blocks, previous, taps, table):
    inputs, block = blocks[0].shape
    rows = inputs * (block // FRAME)
    on_chip = pl.BlockSpec(memory_space=pltpu.VMEM)
    near, far = (*blocks, taps), (previous, table)
    return pl.pallas_call(
        channelize_kernel,
        out_shape=jax.ShapeDtypeStruct((AXES["half"], 2 * table.shape[1], rows), jnp.bfloat16),
        in_specs=[pl.BlockSpec(memory_space=pltpu.SMEM)]
        + [on_chip] * len(near)
        + [pl.BlockSpec(memory_space=pltpu.HBM)] * len(far),
        out_specs=on_chip,
        scratch_shapes=[pltpu.VMEM((2, rows, FRAME // 2), jnp.bfloat16)]
        + [pltpu.VMEM(a.shape, a.dtype) for a in far]
        + [pltpu.SemaphoreType.DMA((len(far),))],
        compiler_params=pltpu.CompilerParams(vmem_limit_bytes=VMEM_BYTES),
    )(place, *near, *far)


def correlate_kernel(inputs, scale, place_ref, received, out, every, own):
    channels, rows, lanes = received.shape
    halves, count = AXES["half"], AXES["y"]
    wide = rows // (halves * count)
    sign = jnp.where(lax.broadcasted_iota(jnp.int32, (inputs, wide), 1) < wide // 2, 1.0, -1.0)
    for k in range(channels):
        for half in range(halves):
            for y in range(count):
                first = (half * count + y) * wide
                turned = received[k, first : first + wide, :].T
                row = (y * halves + half) * inputs
                for s in range(lanes // inputs):
                    at = slice(s * wide, (s + 1) * wide)
                    every[k, row : row + inputs, at] = turned[s * inputs : (s + 1) * inputs]
        for y in range(count):
            row = pl.multiple_of((y * halves + place_ref[2]) * inputs, inputs)
            for s in range(lanes // inputs):
                at = slice(s * wide, (s + 1) * wide)
                part = every[k, pl.ds(row, inputs), at]
                own[k, y * inputs : (y + 1) * inputs, at] = part
                part = pltpu.roll(part.astype(jnp.float32), wide // 2, 1) * sign
                own[k, (count + y) * inputs : (count + y + 1) * inputs, at] = part.astype(jnp.bfloat16)
    for k in range(channels):
        sums = lax.dot_general(
            own[k], every[k], (((1,), (1,)), ((), ())), preferred_element_type=jnp.float32
        )
        sums = (sums * scale).astype(jnp.bfloat16)
        for part in range(2):
            for y in range(count):
                row = (part * count + y) * inputs
                out[y, part, k] = sums[row : row + inputs]


def correlate(place, received, inputs, scale):
    channels, rows, lanes = received.shape
    count, total = AXES["y"], AXES["y"] * AXES["half"] * inputs
    depth = rows * lanes // total
    return pl.pallas_call(
        functools.partial(correlate_kernel, inputs, scale),
        out_shape=jax.ShapeDtypeStruct((count, 2, channels, inputs, total), jnp.bfloat16),
        in_specs=[pl.BlockSpec(memory_space=pltpu.SMEM), pl.BlockSpec(memory_space=pltpu.VMEM)],
        out_specs=pl.BlockSpec(memory_space=pltpu.VMEM),
        scratch_shapes=[pltpu.VMEM((channels, total, depth), jnp.bfloat16)] * 2,
        compiler_params=pltpu.CompilerParams(vmem_limit_bytes=32 * 2**20),
    )(place, received)


def widen_kernel(result, out, wide, sent):
    count, parts, channels = result.shape[:3]
    copies = []
    for part in range(parts):
        for k in range(channels):
            for y in range(count):
                wide[part, k * count + y] = result[y, part, k].astype(jnp.float32)
            at = pl.ds(k * count, count)
            copy = pltpu.make_async_copy(wide.at[part, at], out.at[part, at], sent.at[part * channels + k])
            copy.start()
            copies.append(copy)
    for copy in copies:
        copy.wait()


def widen(result):
    count, parts, channels, inputs, total = result.shape
    shape = (parts, channels * count, inputs, total)
    return pl.pallas_call(
        widen_kernel,
        out_shape=jax.ShapeDtypeStruct(shape, jnp.float32),
        in_specs=[pl.BlockSpec(memory_space=pltpu.VMEM)],
        out_specs=pl.BlockSpec(memory_space=pl.ANY),
        scratch_shapes=[pltpu.VMEM(shape, jnp.float32), pltpu.SemaphoreType.DMA((parts * channels,))],
        compiler_params=pltpu.CompilerParams(vmem_limit_bytes=16 * 2**20),
    )(result)


def body(table, voltages, previous, filter_taps):
    inputs, block = voltages.shape
    here = block // FRAME
    chips, cores = math.prod(AXES[a] for a in CHIP), AXES["core"]
    chip, core = lax.axis_index(CHIP), lax.axis_index("core")
    up = [(c, c + 1) for c in range(chips - 2)]
    down = [(c, (c - 1) % chips) for c in range(chips)]
    route = lambda steps, core: [(a * cores + core, b * cores + core) for a, b in steps]
    first = lax.ppermute(voltages, TIME, route(up, 1) + route(down, 0))
    second = lax.ppermute(voltages, TIME, route(up, 0) + route(down, 1))
    mine, first = lax.optimization_barrier((voltages, first))
    passed = lax.ppermute(first, "core", [(0, 1), (1, 0)])
    swapped = lax.ppermute(mine, "core", [(0, 1), (1, 0)])
    start = (chip * cores + core) * here + AHEAD - REACH - jnp.where(chip == chips - 1, chips * cores * here, 0)
    place = jnp.stack([start, core, lax.axis_index("half")]).astype(jnp.int32)
    own, taps = load(voltages, filter_taps)
    spectra = channelize(place, (own, swapped, first, passed, second), previous, taps, table)
    rows = spectra.shape[2]
    devices = math.prod(AXES.values())
    received = lax.all_to_all(spectra.reshape(devices, CHANNELS * 2, rows), ORDER, 0, 0, tiled=True)
    received = received.reshape(*(AXES[a] for a in ORDER), CHANNELS, 2, rows)
    received = received.transpose(5, 0, 3, 6, 1, 2, 4, 7).reshape(CHANNELS, -1, rows)
    result = correlate(place, received, inputs, FRAME / (chips * cores * block))
    result = lax.all_to_all(result, "y", 0, 0, tiled=True)
    return widen(result)


def solution(mesh):
    parts = Mesh(mesh.devices.reshape(tuple(AXES.values())), tuple(AXES))
    table = dft_table()
    placed = (P(FEED, TIME), P(FEED, None), P())

    def run(voltages, previous, filter_taps):
        return jax.shard_map(
            functools.partial(body, jnp.asarray(table)),
            mesh=parts,
            in_specs=placed,
            out_specs=P(None, TIME, FEED, None),
            check_vma=False,
        )(voltages, previous, filter_taps)

    return run
```

```python
import functools
import math

import jax
import jax.numpy as jnp
import ml_dtypes
import numpy as np
from jax import lax
from jax.experimental import pallas as pl
from jax.experimental.pallas import tpu as pltpu
from jax.sharding import Mesh
from jax.sharding import PartitionSpec as P

FRAME = 2048
HALF = FRAME // 2
TAPS = 16
REACH = TAPS - 1
AHEAD = 8
STEPS = 2
VMEM_BYTES = 50 * 2**20
LOAD_BYTES = 4 * 2**20


AXES = {"y": 4, "half": 2, "x": 4, "z": 8, "core": 2}
FEED = ("y", "half")
TIME = ("x", "z", "core")
CHIP = ("x", "z")
ORDER = ("half", "core", "x", "y", "z")
CHANNELS = 4
BLOCK = AXES["z"] * CHANNELS * 2


def dft_table():
    parity = np.arange(2).reshape(2, 1, 1, 1, 1, 1)
    core = np.arange(2).reshape(1, 2, 1, 1, 1, 1)
    x = np.arange(4).reshape(1, 1, 4, 1, 1, 1)
    upper = np.arange(2).reshape(1, 1, 1, 2, 1, 1)
    z = np.arange(8).reshape(1, 1, 1, 1, 8, 1)
    own = np.arange(CHANNELS).reshape(1, 1, 1, 1, 1, CHANNELS)
    channel = ((x * 8 + z) * 2 + core) * 16 + own * 4 + upper * 2 + parity
    turns = (channel.reshape(-1, 1) * np.arange(FRAME // 2)[None, :]) % FRAME
    angle = turns * (2.0 * math.pi / FRAME)
    table = np.stack([np.cos(angle), -np.sin(angle)], axis=1)
    return table.reshape(2, HALF, FRAME // 2).astype(ml_dtypes.bfloat16)


def load_kernel(count, *refs):
    copies = [pltpu.make_async_copy(refs[i], refs[count + i], refs[-1].at[i]) for i in range(count)]
    for copy in copies:
        copy.start()
    for copy in copies:
        copy.wait()


def load(*arrays):
    count = len(arrays)
    return pl.pallas_call(
        functools.partial(load_kernel, count),
        out_shape=tuple(jax.ShapeDtypeStruct(a.shape, a.dtype) for a in arrays),
        in_specs=[pl.BlockSpec(memory_space=pl.ANY)] * count,
        out_specs=(pl.BlockSpec(memory_space=pltpu.VMEM),) * count,
        scratch_shapes=[pltpu.SemaphoreType.DMA((count,))],
        compiler_params=pltpu.CompilerParams(vmem_limit_bytes=LOAD_BYTES),
    )(*arrays)


def channelize_kernel(place_ref, own, swapped, first, passed, second, taps, far_previous, far_table, out, folded, previous, table, arrived):
    inputs, block = own.shape
    here = block // FRAME
    start = place_ref[0]

    @pl.when(start < 0)
    def _():
        copy = pltpu.make_async_copy(far_previous, previous, arrived.at[1])
        copy.start()
        copy.wait()

    table_copy = pltpu.make_async_copy(far_table, table, arrived.at[0])
    table_copy.start()

    def filter_frames(sources):
        held = [jnp.clip(start + w + REACH, 0, REACH - 1) * FRAME for w in range(REACH)]

        def columns(j, carry):
            for row in range(0, inputs, 16):
                parts = []
                for part in range(2):
                    lane = pl.multiple_of(part * (FRAME // 2) + j * 128, 128)
                    weights = [taps[t : t + 1, pl.ds(lane, 128)] for t in range(TAPS)]
                    frames = []
                    for w in range(here + REACH):
                        source, frame = sources[(w + 1) // here], (w + 1) % here
                        at = pl.ds(pl.multiple_of(frame * FRAME + lane, 128), 128)
                        value = source[row : row + 16, at].astype(jnp.float32)
                        if w < REACH:
                            at = pl.ds(pl.multiple_of(held[w] + lane, 128), 128)
                            old = previous[row : row + 16, at].astype(jnp.float32)
                            value = jnp.where(start + w < 0, old, value)
                        frames.append(value)
                    totals = []
                    for s in range(here):
                        total = weights[0] * frames[s]
                        for t in range(1, TAPS):
                            total = total + weights[t] * frames[s + t]
                        totals.append(total)
                    parts.append(totals)
                at = pl.ds(pl.multiple_of(j * 128, 128), 128)
                for s, (low, high) in enumerate(zip(*parts)):
                    rows = pl.ds(s * inputs + row, 16)
                    folded[0, rows, at] = (low + high).astype(jnp.bfloat16)
                    folded[1, rows, at] = (low - high).astype(jnp.bfloat16)
            return carry

        lax.fori_loop(0, FRAME // 2 // 128, columns, 0)

    @pl.when(place_ref[1] == 0)
    def _():
        filter_frames((second, passed, own, swapped, first))

    @pl.when(place_ref[1] == 1)
    def _():
        filter_frames((first, swapped, own, passed, second))

    table_copy.wait()
    step = table.shape[1] // STEPS
    for parity in range(2):
        for j in range(STEPS):
            spectrum = lax.dot_general(
                table[parity, j * step : (j + 1) * step, :],
                folded[parity],
                (((1,), (1,)), ((), ())),
                preferred_element_type=jnp.float32,
            )
            spectrum = (spectrum * (1.0 / math.sqrt(FRAME))).astype(jnp.bfloat16)
            for block in range(step // BLOCK):
                row = ((j * (step // BLOCK) + block) * 2 + parity) * BLOCK
                for half in range(out.shape[0]):
                    out[half, row : row + BLOCK, :] = spectrum[block * BLOCK : (block + 1) * BLOCK]


def channelize(place, blocks, previous, taps, table):
    inputs, block = blocks[0].shape
    rows = inputs * (block // FRAME)
    on_chip = pl.BlockSpec(memory_space=pltpu.VMEM)
    near, far = (*blocks, taps), (previous, table)
    return pl.pallas_call(
        channelize_kernel,
        out_shape=jax.ShapeDtypeStruct((AXES["half"], 2 * table.shape[1], rows), jnp.bfloat16),
        in_specs=[pl.BlockSpec(memory_space=pltpu.SMEM)]
        + [on_chip] * len(near)
        + [pl.BlockSpec(memory_space=pltpu.HBM)] * len(far),
        out_specs=on_chip,
        scratch_shapes=[pltpu.VMEM((2, rows, FRAME // 2), jnp.bfloat16)]
        + [pltpu.VMEM(a.shape, a.dtype) for a in far]
        + [pltpu.SemaphoreType.DMA((len(far),))],
        compiler_params=pltpu.CompilerParams(vmem_limit_bytes=VMEM_BYTES),
    )(place, *near, *far)


def correlate_kernel(inputs, scale, place_ref, received, out, every, own):
    channels, rows, lanes = received.shape
    halves, count = AXES["half"], AXES["y"]
    wide = rows // (halves * count)
    sign = jnp.where(lax.broadcasted_iota(jnp.int32, (inputs, wide), 1) < wide // 2, 1.0, -1.0)
    for k in range(channels):
        for half in range(halves):
            for y in range(count):
                first = (half * count + y) * wide
                turned = received[k, first : first + wide, :].T
                row = (y * halves + half) * inputs
                for s in range(lanes // inputs):
                    at = slice(s * wide, (s + 1) * wide)
                    every[k, row : row + inputs, at] = turned[s * inputs : (s + 1) * inputs]
        for y in range(count):
            row = pl.multiple_of((y * halves + place_ref[2]) * inputs, inputs)
            for s in range(lanes // inputs):
                at = slice(s * wide, (s + 1) * wide)
                part = every[k, pl.ds(row, inputs), at]
                own[k, y * inputs : (y + 1) * inputs, at] = part
                part = pltpu.roll(part.astype(jnp.float32), wide // 2, 1) * sign
                own[k, (count + y) * inputs : (count + y + 1) * inputs, at] = part.astype(jnp.bfloat16)
    for k in range(channels):
        sums = lax.dot_general(
            own[k], every[k], (((1,), (1,)), ((), ())), preferred_element_type=jnp.float32
        )
        sums = (sums * scale).astype(jnp.bfloat16)
        for part in range(2):
            for y in range(count):
                row = (part * count + y) * inputs
                out[y, part, k] = sums[row : row + inputs]


def correlate(place, received, inputs, scale):
    channels, rows, lanes = received.shape
    count, total = AXES["y"], AXES["y"] * AXES["half"] * inputs
    depth = rows * lanes // total
    return pl.pallas_call(
        functools.partial(correlate_kernel, inputs, scale),
        out_shape=jax.ShapeDtypeStruct((count, 2, channels, inputs, total), jnp.bfloat16),
        in_specs=[pl.BlockSpec(memory_space=pltpu.SMEM), pl.BlockSpec(memory_space=pltpu.VMEM)],
        out_specs=pl.BlockSpec(memory_space=pltpu.VMEM),
        scratch_shapes=[pltpu.VMEM((channels, total, depth), jnp.bfloat16)] * 2,
        compiler_params=pltpu.CompilerParams(vmem_limit_bytes=32 * 2**20),
    )(place, received)


def widen_kernel(result, out, wide, sent):
    count, parts, channels = result.shape[:3]
    copies = []
    for part in range(parts):
        for k in range(channels):
            for y in range(count):
                wide[part, k * count + y] = result[y, part, k].astype(jnp.float32)
            at = pl.ds(k * count, count)
            copy = pltpu.make_async_copy(wide.at[part, at], out.at[part, at], sent.at[part * channels + k])
            copy.start()
            copies.append(copy)
    for copy in copies:
        copy.wait()


def widen(result):
    count, parts, channels, inputs, total = result.shape
    shape = (parts, channels * count, inputs, total)
    return pl.pallas_call(
        widen_kernel,
        out_shape=jax.ShapeDtypeStruct(shape, jnp.float32),
        in_specs=[pl.BlockSpec(memory_space=pltpu.VMEM)],
        out_specs=pl.BlockSpec(memory_space=pl.ANY),
        scratch_shapes=[pltpu.VMEM(shape, jnp.float32), pltpu.SemaphoreType.DMA((parts * channels,))],
        compiler_params=pltpu.CompilerParams(vmem_limit_bytes=16 * 2**20),
    )(result)


def body(table, voltages, previous, filter_taps):
    inputs, block = voltages.shape
    here = block // FRAME
    chips, cores = math.prod(AXES[a] for a in CHIP), AXES["core"]
    chip, core = lax.axis_index(CHIP), lax.axis_index("core")
    up = [(c, c + 1) for c in range(chips - 2)]
    down = [(c, (c - 1) % chips) for c in range(chips)]
    route = lambda steps, core: [(a * cores + core, b * cores + core) for a, b in steps]
    first = lax.ppermute(voltages, TIME, route(up, 1) + route(down, 0))
    second = lax.ppermute(voltages, TIME, route(up, 0) + route(down, 1))
    own, taps = load(voltages, filter_taps)
    swapped = lax.ppermute(own, "core", [(0, 1), (1, 0)])
    passed = lax.ppermute(first, "core", [(0, 1), (1, 0)])
    start = (chip * cores + core) * here + AHEAD - REACH - jnp.where(chip == chips - 1, chips * cores * here, 0)
    place = jnp.stack([start, core, lax.axis_index("half")]).astype(jnp.int32)
    spectra = channelize(place, (own, swapped, first, passed, second), previous, taps, table)
    rows = spectra.shape[2]
    devices = math.prod(AXES.values())
    received = lax.all_to_all(spectra.reshape(devices, CHANNELS * 2, rows), ORDER, 0, 0, tiled=True)
    received = received.reshape(*(AXES[a] for a in ORDER), CHANNELS, 2, rows)
    received = received.transpose(5, 0, 3, 6, 1, 2, 4, 7).reshape(CHANNELS, -1, rows)
    result = correlate(place, received, inputs, FRAME / (chips * cores * block))
    result = lax.all_to_all(result, "y", 0, 0, tiled=True)
    return widen(result)


def solution(mesh):
    parts = Mesh(mesh.devices.reshape(tuple(AXES.values())), tuple(AXES))
    table = dft_table()
    placed = (P(FEED, TIME), P(FEED, None), P())

    def run(voltages, previous, filter_taps):
        return jax.shard_map(
            functools.partial(body, jnp.asarray(table)),
            mesh=parts,
            in_specs=placed,
            out_specs=P(None, TIME, FEED, None),
            check_vma=False,
        )(voltages, previous, filter_taps)

    return run
```

```python
import functools
import math

import jax
import jax.numpy as jnp
import ml_dtypes
import numpy as np
from jax import lax
from jax.experimental import pallas as pl
from jax.experimental.pallas import tpu as pltpu
from jax.sharding import Mesh
from jax.sharding import PartitionSpec as P

FRAME = 2048
HALF = FRAME // 2
TAPS = 16
REACH = TAPS - 1
AHEAD = 8
STEPS = 2
VMEM_BYTES = 50 * 2**20
LOAD_BYTES = 4 * 2**20


AXES = {"y": 4, "half": 2, "x": 4, "z": 8, "core": 2}
FEED = ("y", "half")
TIME = ("x", "z", "core")
CHIP = ("x", "z")
ORDER = ("half", "core", "x", "y", "z")
CHANNELS = 4
BLOCK = AXES["z"] * CHANNELS * 2


def dft_tables():
    core = np.arange(2).reshape(2, 1, 1, 1, 1, 1)
    x = np.arange(4).reshape(1, 4, 1, 1, 1, 1)
    upper = np.arange(2).reshape(1, 1, 2, 1, 1, 1)
    z = np.arange(8).reshape(1, 1, 1, 8, 1, 1)
    own = np.arange(CHANNELS).reshape(1, 1, 1, 1, CHANNELS, 1)
    even = ((x * 8 + z) * 2 + core) * 16 + own * 4 + upper * 2

    def table(channel, count):
        angle = channel * np.arange(count) % FRAME * (2.0 * math.pi / FRAME)
        return np.stack([np.cos(angle), -np.sin(angle)], axis=-2).astype(ml_dtypes.bfloat16)

    odd_table = table(even + 1, FRAME // 2).reshape(HALF, FRAME // 2)
    even_table = np.moveaxis(table(even, FRAME // 4), 2, 0).reshape(2, HALF // 2, FRAME // 4)
    return odd_table, even_table


def load_kernel(count, *refs):
    copies = [pltpu.make_async_copy(refs[i], refs[count + i], refs[-1].at[i]) for i in range(count)]
    for copy in copies:
        copy.start()
    for copy in copies:
        copy.wait()


def load(*arrays):
    count = len(arrays)
    return pl.pallas_call(
        functools.partial(load_kernel, count),
        out_shape=tuple(jax.ShapeDtypeStruct(a.shape, a.dtype) for a in arrays),
        in_specs=[pl.BlockSpec(memory_space=pl.ANY)] * count,
        out_specs=(pl.BlockSpec(memory_space=pltpu.VMEM),) * count,
        scratch_shapes=[pltpu.SemaphoreType.DMA((count,))],
        compiler_params=pltpu.CompilerParams(vmem_limit_bytes=LOAD_BYTES),
    )(*arrays)


def channelize_kernel(place_ref, own, swapped, first, passed, second, taps, far_previous, far_odd, far_even, out, folded, previous, odd, even, arrived):
    inputs, block = own.shape
    here = block // FRAME
    start = place_ref[0]

    @pl.when(start < 0)
    def _():
        copy = pltpu.make_async_copy(far_previous, previous, arrived.at[1])
        copy.start()
        copy.wait()

    odd_copy = pltpu.make_async_copy(far_odd, odd, arrived.at[0])
    even_copy = pltpu.make_async_copy(far_even, even, arrived.at[2])
    odd_copy.start()
    even_copy.start()

    def filter_frames(sources):
        held = [jnp.clip(start + w + REACH, 0, REACH - 1) * FRAME for w in range(REACH)]

        def columns(j, carry):
            for row in range(0, inputs, 16):
                parts = []
                for part in range(4):
                    lane = pl.multiple_of(part * (FRAME // 4) + j * 128, 128)
                    weights = [taps[t : t + 1, pl.ds(lane, 128)] for t in range(TAPS)]
                    frames = []
                    for w in range(here + REACH):
                        source, frame = sources[(w + 1) // here], (w + 1) % here
                        at = pl.ds(pl.multiple_of(frame * FRAME + lane, 128), 128)
                        value = source[row : row + 16, at].astype(jnp.float32)
                        if w < REACH:
                            at = pl.ds(pl.multiple_of(held[w] + lane, 128), 128)
                            old = previous[row : row + 16, at].astype(jnp.float32)
                            value = jnp.where(start + w < 0, old, value)
                        frames.append(value)
                    totals = []
                    for s in range(here):
                        total = weights[0] * frames[s]
                        for t in range(1, TAPS):
                            total = total + weights[t] * frames[s + t]
                        totals.append(total)
                    parts.append(totals)
                at, later = (pl.ds(pl.multiple_of(j * 128 + k * FRAME // 4, 128), 128) for k in range(2))
                for s, (first, second, third, fourth) in enumerate(zip(*parts)):
                    rows = pl.ds(s * inputs + row, 16)
                    folded[1, rows, at] = (first - third).astype(jnp.bfloat16)
                    folded[1, rows, later] = (second - fourth).astype(jnp.bfloat16)
                    first, second = first + third, second + fourth
                    folded[0, rows, at] = (first + second).astype(jnp.bfloat16)
                    folded[0, rows, later] = (first - second).astype(jnp.bfloat16)
            return carry

        lax.fori_loop(0, FRAME // 4 // 128, columns, 0)

    @pl.when(place_ref[1] == 0)
    def _():
        filter_frames((second, passed, own, swapped, first))

    @pl.when(place_ref[1] == 1)
    def _():
        filter_frames((first, swapped, own, passed, second))

    def transform(table, frames):
        spectrum = lax.dot_general(
            table, frames, (((1,), (1,)), ((), ())), preferred_element_type=jnp.float32
        )
        return (spectrum * (1.0 / math.sqrt(FRAME))).astype(jnp.bfloat16)

    def put(spectrum, first, stride):
        for block in range(spectrum.shape[0] // BLOCK):
            row = (first + block * stride) * BLOCK
            for half in range(out.shape[0]):
                out[half, row : row + BLOCK, :] = spectrum[block * BLOCK : (block + 1) * BLOCK]

    odd_copy.wait()
    even_copy.wait()
    step = HALF // STEPS
    for j in range(STEPS):
        put(transform(odd[j * step : (j + 1) * step, :], folded[1]), j * step // BLOCK * 2 + 1, 2)
    for upper in range(2):
        at = slice(upper * FRAME // 4, (upper + 1) * FRAME // 4)
        put(transform(even[upper], folded[0, :, at]), upper * 2, 4)


def channelize(place, blocks, previous, taps, tables):
    inputs, block = blocks[0].shape
    rows = inputs * (block // FRAME)
    on_chip = pl.BlockSpec(memory_space=pltpu.VMEM)
    near, far = (*blocks, taps), (previous, *tables)
    return pl.pallas_call(
        channelize_kernel,
        out_shape=jax.ShapeDtypeStruct((AXES["half"], 2 * HALF, rows), jnp.bfloat16),
        in_specs=[pl.BlockSpec(memory_space=pltpu.SMEM)]
        + [on_chip] * len(near)
        + [pl.BlockSpec(memory_space=pltpu.HBM)] * len(far),
        out_specs=on_chip,
        scratch_shapes=[pltpu.VMEM((2, rows, FRAME // 2), jnp.bfloat16)]
        + [pltpu.VMEM(a.shape, a.dtype) for a in far]
        + [pltpu.SemaphoreType.DMA((len(far),))],
        compiler_params=pltpu.CompilerParams(vmem_limit_bytes=VMEM_BYTES),
    )(place, *near, *far)


def correlate_kernel(inputs, scale, place_ref, received, out, every, own):
    channels, rows, lanes = received.shape
    halves, count = AXES["half"], AXES["y"]
    wide = rows // (halves * count)
    sign = jnp.where(lax.broadcasted_iota(jnp.int32, (inputs, wide), 1) < wide // 2, 1.0, -1.0)
    for k in range(channels):
        for half in range(halves):
            for y in range(count):
                first = (half * count + y) * wide
                turned = received[k, first : first + wide, :].T
                row = (y * halves + half) * inputs
                for s in range(lanes // inputs):
                    at = slice(s * wide, (s + 1) * wide)
                    every[k, row : row + inputs, at] = turned[s * inputs : (s + 1) * inputs]
        for y in range(count):
            row = pl.multiple_of((y * halves + place_ref[2]) * inputs, inputs)
            for s in range(lanes // inputs):
                at = slice(s * wide, (s + 1) * wide)
                part = every[k, pl.ds(row, inputs), at]
                own[k, y * inputs : (y + 1) * inputs, at] = part
                part = pltpu.roll(part.astype(jnp.float32), wide // 2, 1) * sign
                own[k, (count + y) * inputs : (count + y + 1) * inputs, at] = part.astype(jnp.bfloat16)
    for k in range(channels):
        sums = lax.dot_general(
            own[k], every[k], (((1,), (1,)), ((), ())), preferred_element_type=jnp.float32
        )
        sums = (sums * scale).astype(jnp.bfloat16)
        for part in range(2):
            for y in range(count):
                row = (part * count + y) * inputs
                out[y, part, k] = sums[row : row + inputs]


def correlate(place, received, inputs, scale):
    channels, rows, lanes = received.shape
    count, total = AXES["y"], AXES["y"] * AXES["half"] * inputs
    depth = rows * lanes // total
    return pl.pallas_call(
        functools.partial(correlate_kernel, inputs, scale),
        out_shape=jax.ShapeDtypeStruct((count, 2, channels, inputs, total), jnp.bfloat16),
        in_specs=[pl.BlockSpec(memory_space=pltpu.SMEM), pl.BlockSpec(memory_space=pltpu.VMEM)],
        out_specs=pl.BlockSpec(memory_space=pltpu.VMEM),
        scratch_shapes=[pltpu.VMEM((channels, total, depth), jnp.bfloat16)] * 2,
        compiler_params=pltpu.CompilerParams(vmem_limit_bytes=32 * 2**20),
    )(place, received)


def widen_kernel(result, out, wide, sent):
    count, parts, channels = result.shape[:3]
    copies = []
    for part in range(parts):
        for k in range(channels):
            for y in range(count):
                wide[part, k * count + y] = result[y, part, k].astype(jnp.float32)
            at = pl.ds(k * count, count)
            copy = pltpu.make_async_copy(wide.at[part, at], out.at[part, at], sent.at[part * channels + k])
            copy.start()
            copies.append(copy)
    for copy in copies:
        copy.wait()


def widen(result):
    count, parts, channels, inputs, total = result.shape
    shape = (parts, channels * count, inputs, total)
    return pl.pallas_call(
        widen_kernel,
        out_shape=jax.ShapeDtypeStruct(shape, jnp.float32),
        in_specs=[pl.BlockSpec(memory_space=pltpu.VMEM)],
        out_specs=pl.BlockSpec(memory_space=pl.ANY),
        scratch_shapes=[pltpu.VMEM(shape, jnp.float32), pltpu.SemaphoreType.DMA((parts * channels,))],
        compiler_params=pltpu.CompilerParams(vmem_limit_bytes=16 * 2**20),
    )(result)


def body(tables, voltages, previous, filter_taps):
    inputs, block = voltages.shape
    here = block // FRAME
    chips, cores = math.prod(AXES[a] for a in CHIP), AXES["core"]
    chip, core = lax.axis_index(CHIP), lax.axis_index("core")
    up = [(c, c + 1) for c in range(chips - 2)]
    down = [(c, (c - 1) % chips) for c in range(chips)]
    route = lambda steps, core: [(a * cores + core, b * cores + core) for a, b in steps]
    first = lax.ppermute(voltages, TIME, route(up, 1) + route(down, 0))
    second = lax.ppermute(voltages, TIME, route(up, 0) + route(down, 1))
    own, taps = load(voltages, filter_taps)
    swapped = lax.ppermute(own, "core", [(0, 1), (1, 0)])
    passed = lax.ppermute(first, "core", [(0, 1), (1, 0)])
    start = (chip * cores + core) * here + AHEAD - REACH - jnp.where(chip == chips - 1, chips * cores * here, 0)
    place = jnp.stack([start, core, lax.axis_index("half")]).astype(jnp.int32)
    spectra = channelize(place, (own, swapped, first, passed, second), previous, taps, tables)
    rows = spectra.shape[2]
    devices = math.prod(AXES.values())
    received = lax.all_to_all(spectra.reshape(devices, CHANNELS * 2, rows), ORDER, 0, 0, tiled=True)
    received = received.reshape(*(AXES[a] for a in ORDER), CHANNELS, 2, rows)
    received = received.transpose(5, 0, 3, 6, 1, 2, 4, 7).reshape(CHANNELS, -1, rows)
    result = correlate(place, received, inputs, FRAME / (chips * cores * block))
    result = lax.all_to_all(result, "y", 0, 0, tiled=True)
    return widen(result)


def solution(mesh):
    parts = Mesh(mesh.devices.reshape(tuple(AXES.values())), tuple(AXES))
    tables = dft_tables()
    placed = (P(FEED, TIME), P(FEED, None), P())

    def run(voltages, previous, filter_taps):
        return jax.shard_map(
            functools.partial(body, tuple(jnp.asarray(table) for table in tables)),
            mesh=parts,
            in_specs=placed,
            out_specs=P(None, TIME, FEED, None),
            check_vma=False,
        )(voltages, previous, filter_taps)

    return run
```

```python
import functools
import math

import jax
import jax.numpy as jnp
import ml_dtypes
import numpy as np
from jax import lax
from jax.experimental import pallas as pl
from jax.experimental.pallas import tpu as pltpu
from jax.sharding import Mesh
from jax.sharding import PartitionSpec as P

FRAME = 2048
HALF = FRAME // 2
TAPS = 16
REACH = TAPS - 1
AHEAD = 8
STEPS = 2
VMEM_BYTES = 50 * 2**20
LOAD_BYTES = 4 * 2**20


AXES = {"y": 4, "half": 2, "x": 4, "z": 8, "core": 2}
FEED = ("y", "half")
TIME = ("x", "z", "core")
CHIP = ("x", "z")
ORDER = ("half", "core", "x", "y", "z")
CHANNELS = 4
BLOCK = AXES["z"] * CHANNELS * 2


def dft_tables():
    core = np.arange(2).reshape(2, 1, 1, 1, 1, 1)
    x = np.arange(4).reshape(1, 4, 1, 1, 1, 1)
    upper = np.arange(2).reshape(1, 1, 2, 1, 1, 1)
    z = np.arange(8).reshape(1, 1, 1, 8, 1, 1)
    own = np.arange(CHANNELS).reshape(1, 1, 1, 1, CHANNELS, 1)
    even = ((x * 8 + z) * 2 + core) * 16 + own * 4 + upper * 2

    def table(channel, count):
        angle = channel * np.arange(count) % FRAME * (2.0 * math.pi / FRAME)
        return np.stack([np.cos(angle), -np.sin(angle)], axis=-2).astype(ml_dtypes.bfloat16)

    odd_table = table(even + 1, FRAME // 2).reshape(HALF, FRAME // 2)
    even_table = np.moveaxis(table(even, FRAME // 4), 2, 0).reshape(2, HALF // 2, FRAME // 4)
    return odd_table, even_table


def load_kernel(count, *refs):
    copies = [pltpu.make_async_copy(refs[i], refs[count + i], refs[-1].at[i]) for i in range(count)]
    for copy in copies:
        copy.start()
    for copy in copies:
        copy.wait()


def load(*arrays):
    count = len(arrays)
    return pl.pallas_call(
        functools.partial(load_kernel, count),
        out_shape=tuple(jax.ShapeDtypeStruct(a.shape, a.dtype) for a in arrays),
        in_specs=[pl.BlockSpec(memory_space=pl.ANY)] * count,
        out_specs=(pl.BlockSpec(memory_space=pltpu.VMEM),) * count,
        scratch_shapes=[pltpu.SemaphoreType.DMA((count,))],
        compiler_params=pltpu.CompilerParams(vmem_limit_bytes=LOAD_BYTES),
    )(*arrays)


def channelize_kernel(place_ref, own, swapped, first, passed, second, taps, far_previous, far_odd, far_even, out, folded, previous, odd, even, arrived):
    inputs, block = own.shape
    here = block // FRAME
    start = place_ref[0]

    @pl.when(start < 0)
    def _():
        copy = pltpu.make_async_copy(far_previous, previous, arrived.at[1])
        copy.start()
        copy.wait()

    odd_copy = pltpu.make_async_copy(far_odd, odd, arrived.at[0])
    even_copy = pltpu.make_async_copy(far_even, even, arrived.at[2])
    odd_copy.start()
    even_copy.start()

    def filter_frames(sources):
        held = [jnp.clip(start + w + REACH, 0, REACH - 1) * FRAME for w in range(REACH)]

        def columns(j, carry):
            for row in range(0, inputs, 16):
                parts = []
                for part in range(4):
                    lane = pl.multiple_of(part * (FRAME // 4) + j * 128, 128)
                    weights = [taps[t : t + 1, pl.ds(lane, 128)] for t in range(TAPS)]
                    frames = []
                    for w in range(here + REACH):
                        source, frame = sources[(w + 1) // here], (w + 1) % here
                        at = pl.ds(pl.multiple_of(frame * FRAME + lane, 128), 128)
                        value = source[row : row + 16, at].astype(jnp.float32)
                        if w < REACH:
                            at = pl.ds(pl.multiple_of(held[w] + lane, 128), 128)
                            old = previous[row : row + 16, at].astype(jnp.float32)
                            value = jnp.where(start + w < 0, old, value)
                        frames.append(value)
                    totals = []
                    for s in range(here):
                        total = weights[0] * frames[s]
                        for t in range(1, TAPS):
                            total = total + weights[t] * frames[s + t]
                        totals.append(total)
                    parts.append(totals)
                at, later = (pl.ds(pl.multiple_of(j * 128 + k * FRAME // 4, 128), 128) for k in range(2))
                for s, (first, second, third, fourth) in enumerate(zip(*parts)):
                    rows = pl.ds(s * inputs + row, 16)
                    folded[1, rows, at] = (first - third).astype(jnp.bfloat16)
                    folded[1, rows, later] = (second - fourth).astype(jnp.bfloat16)
                    first, second = first + third, second + fourth
                    folded[0, rows, at] = (first + second).astype(jnp.bfloat16)
                    folded[0, rows, later] = (first - second).astype(jnp.bfloat16)
            return carry

        lax.fori_loop(0, FRAME // 4 // 128, columns, 0, unroll=2)

    @pl.when(place_ref[1] == 0)
    def _():
        filter_frames((second, passed, own, swapped, first))

    @pl.when(place_ref[1] == 1)
    def _():
        filter_frames((first, swapped, own, passed, second))

    def transform(table, frames):
        spectrum = lax.dot_general(
            table, frames, (((1,), (1,)), ((), ())), preferred_element_type=jnp.float32
        )
        return (spectrum * (1.0 / math.sqrt(FRAME))).astype(jnp.bfloat16)

    def put(spectrum, first, stride):
        for block in range(spectrum.shape[0] // BLOCK):
            row = (first + block * stride) * BLOCK
            for half in range(out.shape[0]):
                out[half, row : row + BLOCK, :] = spectrum[block * BLOCK : (block + 1) * BLOCK]

    odd_copy.wait()
    even_copy.wait()
    step = HALF // STEPS
    for j in range(STEPS):
        put(transform(odd[j * step : (j + 1) * step, :], folded[1]), j * step // BLOCK * 2 + 1, 2)
    for upper in range(2):
        at = slice(upper * FRAME // 4, (upper + 1) * FRAME // 4)
        put(transform(even[upper], folded[0, :, at]), upper * 2, 4)


def channelize(place, blocks, previous, taps, tables):
    inputs, block = blocks[0].shape
    rows = inputs * (block // FRAME)
    on_chip = pl.BlockSpec(memory_space=pltpu.VMEM)
    near, far = (*blocks, taps), (previous, *tables)
    return pl.pallas_call(
        channelize_kernel,
        out_shape=jax.ShapeDtypeStruct((AXES["half"], 2 * HALF, rows), jnp.bfloat16),
        in_specs=[pl.BlockSpec(memory_space=pltpu.SMEM)]
        + [on_chip] * len(near)
        + [pl.BlockSpec(memory_space=pltpu.HBM)] * len(far),
        out_specs=on_chip,
        scratch_shapes=[pltpu.VMEM((2, rows, FRAME // 2), jnp.bfloat16)]
        + [pltpu.VMEM(a.shape, a.dtype) for a in far]
        + [pltpu.SemaphoreType.DMA((len(far),))],
        compiler_params=pltpu.CompilerParams(vmem_limit_bytes=VMEM_BYTES),
    )(place, *near, *far)


def correlate_kernel(inputs, scale, place_ref, received, out, every, own):
    channels, rows, lanes = received.shape
    halves, count = AXES["half"], AXES["y"]
    wide = rows // (halves * count)
    sign = jnp.where(lax.broadcasted_iota(jnp.int32, (inputs, wide), 1) < wide // 2, 1.0, -1.0)
    for k in range(channels):
        for half in range(halves):
            for y in range(count):
                first = (half * count + y) * wide
                turned = received[k, first : first + wide, :].T
                row = (y * halves + half) * inputs
                for s in range(lanes // inputs):
                    at = slice(s * wide, (s + 1) * wide)
                    every[k, row : row + inputs, at] = turned[s * inputs : (s + 1) * inputs]
        for y in range(count):
            row = pl.multiple_of((y * halves + place_ref[2]) * inputs, inputs)
            for s in range(lanes // inputs):
                at = slice(s * wide, (s + 1) * wide)
                part = every[k, pl.ds(row, inputs), at]
                own[k, y * inputs : (y + 1) * inputs, at] = part
                part = pltpu.roll(part.astype(jnp.float32), wide // 2, 1) * sign
                own[k, (count + y) * inputs : (count + y + 1) * inputs, at] = part.astype(jnp.bfloat16)
    for k in range(channels):
        sums = lax.dot_general(
            own[k], every[k], (((1,), (1,)), ((), ())), preferred_element_type=jnp.float32
        )
        sums = (sums * scale).astype(jnp.bfloat16)
        for part in range(2):
            for y in range(count):
                row = (part * count + y) * inputs
                out[y, part, k] = sums[row : row + inputs]


def correlate(place, received, inputs, scale):
    channels, rows, lanes = received.shape
    count, total = AXES["y"], AXES["y"] * AXES["half"] * inputs
    depth = rows * lanes // total
    return pl.pallas_call(
        functools.partial(correlate_kernel, inputs, scale),
        out_shape=jax.ShapeDtypeStruct((count, 2, channels, inputs, total), jnp.bfloat16),
        in_specs=[pl.BlockSpec(memory_space=pltpu.SMEM), pl.BlockSpec(memory_space=pltpu.VMEM)],
        out_specs=pl.BlockSpec(memory_space=pltpu.VMEM),
        scratch_shapes=[pltpu.VMEM((channels, total, depth), jnp.bfloat16)] * 2,
        compiler_params=pltpu.CompilerParams(vmem_limit_bytes=32 * 2**20),
    )(place, received)


def widen_kernel(result, out, wide, sent):
    count, parts, channels = result.shape[:3]
    copies = []
    for part in range(parts):
        for k in range(channels):
            for y in range(count):
                wide[part, k * count + y] = result[y, part, k].astype(jnp.float32)
            at = pl.ds(k * count, count)
            copy = pltpu.make_async_copy(wide.at[part, at], out.at[part, at], sent.at[part * channels + k])
            copy.start()
            copies.append(copy)
    for copy in copies:
        copy.wait()


def widen(result):
    count, parts, channels, inputs, total = result.shape
    shape = (parts, channels * count, inputs, total)
    return pl.pallas_call(
        widen_kernel,
        out_shape=jax.ShapeDtypeStruct(shape, jnp.float32),
        in_specs=[pl.BlockSpec(memory_space=pltpu.VMEM)],
        out_specs=pl.BlockSpec(memory_space=pl.ANY),
        scratch_shapes=[pltpu.VMEM(shape, jnp.float32), pltpu.SemaphoreType.DMA((parts * channels,))],
        compiler_params=pltpu.CompilerParams(vmem_limit_bytes=16 * 2**20),
    )(result)


def body(tables, voltages, previous, filter_taps):
    inputs, block = voltages.shape
    here = block // FRAME
    chips, cores = math.prod(AXES[a] for a in CHIP), AXES["core"]
    chip, core = lax.axis_index(CHIP), lax.axis_index("core")
    up = [(c, c + 1) for c in range(chips - 2)]
    down = [(c, (c - 1) % chips) for c in range(chips)]
    route = lambda steps, core: [(a * cores + core, b * cores + core) for a, b in steps]
    first = lax.ppermute(voltages, TIME, route(up, 1) + route(down, 0))
    second = lax.ppermute(voltages, TIME, route(up, 0) + route(down, 1))
    own, taps = load(voltages, filter_taps)
    swapped = lax.ppermute(own, "core", [(0, 1), (1, 0)])
    passed = lax.ppermute(first, "core", [(0, 1), (1, 0)])
    start = (chip * cores + core) * here + AHEAD - REACH - jnp.where(chip == chips - 1, chips * cores * here, 0)
    place = jnp.stack([start, core, lax.axis_index("half")]).astype(jnp.int32)
    spectra = channelize(place, (own, swapped, first, passed, second), previous, taps, tables)
    rows = spectra.shape[2]
    devices = math.prod(AXES.values())
    received = lax.all_to_all(spectra.reshape(devices, CHANNELS * 2, rows), ORDER, 0, 0, tiled=True)
    received = received.reshape(*(AXES[a] for a in ORDER), CHANNELS, 2, rows)
    received = received.transpose(5, 0, 3, 6, 1, 2, 4, 7).reshape(CHANNELS, -1, rows)
    result = correlate(place, received, inputs, FRAME / (chips * cores * block))
    result = lax.all_to_all(result, "y", 0, 0, tiled=True)
    return widen(result)


def solution(mesh):
    parts = Mesh(mesh.devices.reshape(tuple(AXES.values())), tuple(AXES))
    tables = dft_tables()
    placed = (P(FEED, TIME), P(FEED, None), P())

    def run(voltages, previous, filter_taps):
        return jax.shard_map(
            functools.partial(body, tuple(jnp.asarray(table) for table in tables)),
            mesh=parts,
            in_specs=placed,
            out_specs=P(None, TIME, FEED, None),
            check_vma=False,
        )(voltages, previous, filter_taps)

    return run
```
